256 devices in a mesh: energy: 16 (over x, y), kmom: 16 (over z, core).
Axes of the slice: x: 4, y: 4, z: 8, core: 2. Of those that a mesh axis runs over, the one named last changes fastest.
Arguments:
- green_blocks: bfloat16 [32, 16, 144, 2048], P('energy', 'kmom'), may hold values from -6 to 6
- phonon: float32 [2, 8, 16], replicated, may hold values from -0.4 to 0.4
- offsets: int32 [8], replicated, may hold values from 1 to 2, as said below
- neighbours: int32 [2048, 8], P('kmom'), may hold values from 0 to 2047, as said below
- coupling: float32 [8, 12, 12], replicated, may hold values from -1.75 to 1.75
Outputs:
- self_energy: bfloat16 [32, 16, 144, 2048], P('energy', 'kmom')
The draws below stay inside these ranges and needn't reach their ends.
Inputs may be any that keep to these rules, and one draw needn't show every extreme that they name: `offsets`: each value lies in 1 .. 2; at least one equals 2. Every neighbour of atom a lies within 32 of a in index; some atom has neighbours at exactly a + 32 and a - 32.
All inputs are finite; a program needn't handle non-finite values.
Results may differ from the reference program's by a relative error of at most 0.0064.
Values may be sent and summed in bfloat16 or wider, within the bound.
No kernel may reach another device: no remote copies, remote signals or barrier semaphores. Data moves between devices by JAX's collectives and lax.ppermute only.
A program may use at most 64 MiB of HBM per device.

```python
import jax
import jax.numpy as jnp
from jax import lax

NORB = 12
NPAIR = 144
NW = 8
NB = 8
NK = 16
E_DEV = 2
OFFSET = 2
RADIUS = 32
NE = 32
NA = 2048


def draw_offsets(key, part):
    base_values = jax.random.randint(key, (NW,), 1, OFFSET + 1, dtype=jnp.int32)
    chosen = jax.random.randint(jax.random.fold_in(key, 7), (), 0, NW, dtype=jnp.int32)
    places = jnp.arange(NW, dtype=jnp.int32)
    return jnp.where(places == chosen, OFFSET, base_values).astype(jnp.int32)


def draw_neighbours(key, part):
    steps_drawn = jax.random.randint(key, (NA, NB), -RADIUS, RADIUS + 1, dtype=jnp.int32)
    chosen = jax.random.randint(jax.random.fold_in(key, 11), (), RADIUS, NA - RADIUS, dtype=jnp.int32)
    atom_ids = jnp.arange(NA, dtype=jnp.int32)[:, None]
    slot_ids = jnp.arange(NB, dtype=jnp.int32)[None, :]
    steps_drawn = jnp.where((atom_ids == chosen) & (slot_ids == 0), RADIUS, steps_drawn)
    steps_drawn = jnp.where((atom_ids == chosen) & (slot_ids == 1), -RADIUS, steps_drawn)
    return jnp.clip(atom_ids + steps_drawn, 0, NA - 1).astype(jnp.int32)


def steps_of(rng, extent, pieces, least, top_value):
    factor_of, own = 1.0, jax.random.fold_in(rng, 6)
    for axis_at, parts in pieces:
        draws = jnp.exp(jax.random.uniform(jax.random.fold_in(own, axis_at), (parts,), jnp.float32, least / len(pieces), top_value / len(pieces)))
        factor_of = factor_of * jnp.repeat(draws, extent[axis_at] // parts).reshape([-1 if axis == axis_at else 1 for axis in range(len(extent))])
    return factor_of


def scatter_about(rng, shape, deviation, bound, shards=(), kind=jnp.bfloat16):
    entries = deviation * jax.random.normal(rng, shape, jnp.float32)
    if shards:
        entries = entries * steps_of(rng, shape, shards, -0.22, 0.18)
    return jnp.clip(entries, -bound, bound).astype(kind)


def setup_inputs(seed: int = 0) -> dict:
    seeds = jax.random.split(jax.random.key(seed), 6)
    green_blocks = scatter_about(seeds[0], (NE, NK, NPAIR, NA), 1.0, 6.0, ((0, 16), (1, 16)))
    phonon = scatter_about(seeds[1], (2, NW, NK), 0.0625, 0.4, (), jnp.float32)
    offsets = draw_offsets(jax.random.fold_in(seeds[5], 71), 0)
    neighbours = draw_neighbours(jax.random.fold_in(seeds[5], 71), 0)
    coupling = scatter_about(seeds[4], (NB, NORB, NORB), NORB ** -0.5, 1.75, (), jnp.float32)
    return dict(green_blocks=green_blocks, phonon=phonon, offsets=offsets, neighbours=neighbours, coupling=coupling)


def energy_kernel(phonon, offsets, block_rows):
    mom_count = phonon.shape[2]
    rel_values = jnp.arange(2 * OFFSET + 1, dtype=jnp.int32) - OFFSET
    sign_values = jnp.array([-1, 1], dtype=jnp.int32)
    shifts = sign_values[:, None] * offsets[None, :]
    rel_hit = (shifts[:, :, None] == rel_values[None, None, :]).astype(jnp.float32)
    energy_taps = jnp.einsum("swr,swq->rq", rel_hit, phonon.astype(jnp.float32), precision=lax.Precision.HIGHEST)
    energy_taps = energy_taps.astype(jnp.bfloat16).astype(jnp.float32)
    out_rows = jnp.arange(block_rows, dtype=jnp.int32)
    in_rows = jnp.arange(block_rows + 2 * OFFSET, dtype=jnp.int32)
    tap_index = jnp.arange(2 * OFFSET + 1, dtype=jnp.int32)
    row_hit = ((in_rows[None, :, None] - out_rows[:, None, None]) == tap_index[None, None, :]).astype(jnp.float32)
    moms = jnp.arange(mom_count, dtype=jnp.int32)
    mom_hit = (((moms[:, None, None] - moms[None, :, None]) % mom_count) == moms[None, None, :]).astype(jnp.float32)
    kernel = jnp.einsum("abr,kjq,rq->akbj", row_hit, mom_hit, energy_taps, precision=lax.Precision.HIGHEST)
    kernel = kernel.reshape(block_rows * mom_count, (block_rows + 2 * OFFSET) * mom_count)
    return kernel.astype(jnp.bfloat16)


def orbital_pairs(coupling):
    slots = coupling.shape[0]
    orbs = coupling.shape[1]
    outer = jnp.einsum("nip,njr->nijpr", coupling, coupling, precision=lax.Precision.HIGHEST)
    return outer.reshape(slots, orbs * orbs, orbs * orbs).astype(jnp.bfloat16)


def reference(green_blocks, phonon, offsets, neighbours, coupling):
    kernel = energy_kernel(phonon, offsets, E_DEV)
    pair_maps = orbital_pairs(coupling)

    def one_energy(green_row):
        def add_slot(running, scan_item):
            near_atoms, pair_map = scan_item
            taken = jnp.take(green_row, near_atoms, axis=2)
            product = jnp.einsum("kca,dc->kda", taken.astype(jnp.float32), pair_map.astype(jnp.float32))
            return running + product, None

        start_sum = jnp.zeros((NK, NPAIR, NA), jnp.float32)
        running, _ = lax.scan(add_slot, start_sum, (neighbours.T, pair_maps))
        return running.astype(jnp.bfloat16)

    coupled = lax.map(one_energy, green_blocks)
    padded = jnp.pad(coupled, ((OFFSET, OFFSET), (0, 0), (0, 0), (0, 0)))
    tiles = NE // E_DEV

    def one_tile(tile_index):
        first_row = (tile_index * E_DEV).astype(jnp.int32)
        window = lax.dynamic_slice_in_dim(padded, first_row, E_DEV + 2 * OFFSET, 0)
        flat_window = window.reshape((E_DEV + 2 * OFFSET) * NK, NPAIR * NA)
        smeared = jnp.dot(kernel, flat_window, preferred_element_type=jnp.float32).astype(jnp.bfloat16)
        return smeared.reshape(E_DEV, NK, NPAIR, NA)

    result = lax.map(one_tile, jnp.arange(tiles, dtype=jnp.int32))
    return result.reshape(NE, NK, NPAIR, NA)
```

```python
import functools

import jax
import jax.numpy as jnp
from jax import lax
from jax.experimental import pallas as pl
from jax.experimental.pallas import tpu as pltpu
from jax.sharding import Mesh
from jax.sharding import PartitionSpec as P

OFFSET = 2
RADIUS = 32
CHUNKS = 2
ROWS = 16
LANES = 128
KMOM = ("z", "core")
SHIFTS = (4, 3, -3, 2, -2, 1, -1, 0)
VMEM = pl.BlockSpec(memory_space=pltpu.VMEM)
SMEM = pl.BlockSpec(memory_space=pltpu.SMEM)
ROOM = pltpu.CompilerParams(vmem_limit_bytes=40 * 2**20)


def energy_taps(phonon, offsets):
    rel_values = jnp.arange(2 * OFFSET + 1, dtype=jnp.int32) - OFFSET
    sign_values = jnp.array([-1, 1], dtype=jnp.int32)
    shifts = sign_values[:, None] * offsets[None, :]
    rel_hit = (shifts[:, :, None] == rel_values[None, None, :]).astype(jnp.float32)
    taps = jnp.sum(rel_hit[:, :, :, None] * phonon[:, :, None, :], axis=(0, 1))
    return taps.astype(jnp.bfloat16).astype(jnp.float32)


def mixing(taps, core, e_dev, groups):
    moms = taps.shape[1]
    shift = jnp.asarray(SHIFTS, dtype=jnp.int32)
    e_out = jnp.arange(e_dev, dtype=jnp.int32)
    e_in = (jnp.arange(3, dtype=jnp.int32)[:, None] - 1) * e_dev + jnp.arange(e_dev, dtype=jnp.int32)[None, :]
    r = e_in[None] - e_out[:, None, None] + OFFSET
    r_hit = (r[..., None] == jnp.arange(2 * OFFSET + 1, dtype=jnp.int32)).astype(jnp.float32)
    parity = jnp.stack([jnp.int32(0), 1 - 2 * core])
    q = (2 * (shift[None, :, None] + shift[None, None, :]) + parity[:, None, None]) % moms
    q_hit = (q[..., None] == jnp.arange(moms, dtype=jnp.int32)).astype(jnp.float32)
    t = jnp.einsum("otir,rq,pusq->oputsi", r_hit, taps, q_hit, precision=lax.Precision.HIGHEST)
    t = t.reshape(e_dev * 2 * groups, 3 * groups * e_dev)
    eye = jnp.eye(ROWS, dtype=jnp.float32)
    wide = t[:, None, :, None] * eye[None, :, None, :]
    return wide.reshape(t.shape[0] * ROWS, t.shape[1] * ROWS).astype(jnp.bfloat16)


def orbital_pairs(coupling):
    slots, orbs = coupling.shape[0], coupling.shape[1]
    pairs = jnp.arange(orbs * orbs, dtype=jnp.int32)
    orb = jnp.arange(orbs, dtype=jnp.int32)
    first = (pairs[:, None] // orbs == orb[None, :]).astype(jnp.float32)
    second = (pairs[:, None] % orbs == orb[None, :]).astype(jnp.float32)

    def spread(pick):
        half = jnp.einsum("nip,di->dnp", coupling, pick, precision=lax.Precision.HIGHEST)
        return jnp.einsum("dnp,cp->dnc", half, pick, precision=lax.Precision.HIGHEST)

    return (spread(first) * spread(second)).reshape(orbs * orbs, -1).astype(jnp.bfloat16)


def cut_kernel(chunk, groups, z_ref, green_ref, *out_refs):
    width = out_refs[0].shape[2]
    for out, shift in zip(out_refs, SHIFTS):
        group = lax.rem(z_ref[0] + shift + groups, groups)
        start = pl.multiple_of((chunk * groups + group) * width, LANES)
        out[...] = green_ref[:, :, pl.ds(start, width)]


def cut(green, z, chunk, groups):
    e_dev, pairs, atoms = green.shape
    width = atoms // (groups * CHUNKS)
    return pl.pallas_call(
        functools.partial(cut_kernel, chunk, groups),
        out_shape=[jax.ShapeDtypeStruct((e_dev, pairs, width), green.dtype)] * groups,
        in_specs=[SMEM, VMEM],
        out_specs=[VMEM] * groups,
        compiler_params=ROOM,
    )(z, green)


def stack_kernel(*refs):
    out = refs[-1]
    for i, block in enumerate(refs[:-1]):
        out[i] = block[...]


def stack(blocks):
    return pl.pallas_call(
        stack_kernel,
        out_shape=jax.ShapeDtypeStruct((len(blocks), *blocks[0].shape), blocks[0].dtype),
        in_specs=[VMEM] * len(blocks),
        out_specs=VMEM,
        compiler_params=ROOM,
    )(*blocks)


def mix_kernel(mix_ref, low_ref, own_ref, high_ref, same_ref, other_ref):
    groups, e_dev, pairs, width = own_ref.shape
    for g in range(pairs // ROWS):
        rows = pl.ds(g * ROWS, ROWS)
        tiles = [ref[:, :, rows, :].reshape(groups * e_dev * ROWS, width) for ref in (low_ref, own_ref, high_ref)]
        mixed = jnp.dot(mix_ref[...], jnp.concatenate(tiles, axis=0), preferred_element_type=jnp.float32)
        mixed = mixed.reshape(e_dev, 2, groups, ROWS, width)
        for e in range(e_dev):
            same_ref[:, e, rows, :] = mixed[e, 0]
            other_ref[:, e, rows, :] = mixed[e, 1].astype(jnp.bfloat16)


def mix(matrix, low, own, high):
    return pl.pallas_call(
        mix_kernel,
        out_shape=[jax.ShapeDtypeStruct(own.shape, jnp.float32), jax.ShapeDtypeStruct(own.shape, jnp.bfloat16)],
        in_specs=[VMEM] * 4,
        out_specs=[VMEM] * 2,
        compiler_params=ROOM,
    )(matrix, low, own, high)


def add_kernel(same_ref, other_ref, *out_refs):
    for i, out in enumerate(out_refs):
        out[...] = (same_ref[i] + other_ref[i].astype(jnp.float32)).astype(jnp.bfloat16)


def add(same, other):
    groups = same.shape[0]
    return pl.pallas_call(
        add_kernel,
        out_shape=[jax.ShapeDtypeStruct(same.shape[1:], jnp.bfloat16)] * groups,
        in_specs=[VMEM] * 2,
        out_specs=[VMEM] * groups,
        compiler_params=ROOM,
    )(same, other)


def couple_kernel(groups, z_ref, pair_ref, near_ref, *refs):
    blocks, out_ref, line, seen = refs[:-3], refs[-3], refs[-2], refs[-1]
    e_dev, pairs, width = blocks[0].shape
    slots = near_ref.shape[0]
    atoms = out_ref.shape[2]
    span = 2 * LANES
    pad = LANES // 2
    line[:, 0:LANES] = jnp.zeros((e_dev * pairs, LANES), jnp.bfloat16)
    line[:, atoms : atoms + LANES] = jnp.zeros((e_dev * pairs, LANES), jnp.bfloat16)
    for i, block in enumerate(blocks):
        chunk, shift = i // groups, SHIFTS[i % groups]
        group = lax.rem(z_ref[0] - shift + groups, groups)
        start = pl.multiple_of((chunk * groups + group) * width, LANES)
        seen[:, pl.ds(start, width)] = block[...].reshape(e_dev * pairs, width)
    line[:, pad : pad + atoms] = seen[...]
    place = lax.broadcasted_iota(jnp.int32, (span, LANES), 0)

    def step(b, carry):
        start = pl.multiple_of(b * LANES, LANES)
        lanes = pl.ds(start, LANES)
        window = line[:, pl.ds(start, span)]
        base = start - pad
        hits = []
        for n in range(slots):
            near = near_ref[n : n + 1, lanes] - base
            hits.append((place == near).astype(jnp.bfloat16))
        taken = jnp.dot(window, jnp.concatenate(hits, axis=1), preferred_element_type=jnp.float32).astype(jnp.bfloat16)
        columns = [
            jnp.concatenate([taken[e * pairs : (e + 1) * pairs, n * LANES : (n + 1) * LANES] for n in range(slots)], axis=0)
            for e in range(e_dev)
        ]
        total = jnp.dot(pair_ref[...], jnp.concatenate(columns, axis=1), preferred_element_type=jnp.float32)
        for e in range(e_dev):
            out_ref[e, :, lanes] = total[:, e * LANES : (e + 1) * LANES].astype(jnp.bfloat16)
        return carry

    lax.fori_loop(0, atoms // LANES, step, 0)


def couple(blocks, z, pair_maps, near, groups):
    e_dev, pairs, width = blocks[0].shape
    atoms = near.shape[1]
    return pl.pallas_call(
        functools.partial(couple_kernel, groups),
        out_shape=jax.ShapeDtypeStruct((e_dev, pairs, atoms), jnp.bfloat16),
        in_specs=[SMEM] + [VMEM] * (2 + len(blocks)),
        out_specs=VMEM,
        scratch_shapes=[
            pltpu.VMEM((e_dev * pairs, atoms + LANES), jnp.bfloat16),
            pltpu.VMEM((e_dev * pairs, atoms), jnp.bfloat16),
        ],
        compiler_params=ROOM,
    )(z, pair_maps, near, *blocks)


def along_z(x, shift):
    groups = lax.axis_size("z")
    return lax.ppermute(x, "z", [(i, (i + shift) % groups) for i in range(groups)])


def exchange(blocks):
    return [along_z(b, s) if s else b for b, s in zip(blocks, SHIFTS)]


def body(green_blocks, phonon, offsets, neighbours, coupling):
    groups, tiles = lax.axis_size("z"), lax.axis_size("energy")
    z = lax.axis_index("z")[None]
    green = green_blocks[:, 0]
    forward = [(i, i + 1) for i in range(tiles - 1)]
    backward = [(i + 1, i) for i in range(tiles - 1)]
    arrived = [exchange(cut(green, z, c, groups)) for c in range(CHUNKS)]
    matrix = mixing(energy_taps(phonon, offsets), lax.axis_index("core"), green.shape[0], groups)
    near = lax.all_gather(neighbours, KMOM, axis=0, tiled=True).T
    pair_maps = orbital_pairs(coupling)
    back = []
    for blocks in arrived:
        own = stack(blocks)
        low, high = lax.ppermute(own, "energy", forward), lax.ppermute(own, "energy", backward)
        same, other = mix(matrix, low, own, high)
        other = lax.ppermute(other, "core", [(0, 1), (1, 0)])
        back += exchange(add(same, other))
    return couple(back, z, pair_maps, near, groups)[:, None]


def solution(mesh):
    torus = Mesh(mesh.devices.reshape(mesh.shape["energy"], -1, 2), ("energy", *KMOM))
    placed = (P("energy", KMOM, None, None), P(), P(), P(KMOM, None), P())
    return jax.shard_map(body, mesh=torus, in_specs=placed, out_specs=P("energy", KMOM, None, None), check_vma=False)
```

```python
import functools

import jax
import jax.numpy as jnp
import numpy as np
from jax import lax
from jax.experimental import pallas as pl
from jax.experimental.pallas import tpu as pltpu
from jax.sharding import Mesh
from jax.sharding import PartitionSpec as P

OFFSET = 2
TAPS = 2 * OFFSET + 1
CHUNKS = 2
ROWS = 16
LANES = 128
SPAN = 2 * LANES
PAD = LANES // 2
KMOM = ("z", "core")
VMEM = pl.BlockSpec(memory_space=pltpu.VMEM)
SMEM = pl.BlockSpec(memory_space=pltpu.SMEM)
BF16, F32 = jnp.bfloat16, jnp.float32

NEAR = (1, 2, 3)
PLACES = tuple((j, other) for j in NEAR for other in (0, 1)) + ((4, 0), (0, 0))


def call(kernel, outs, *args, scratch=(), cost=None):
    return pl.pallas_call(
        kernel,
        out_shape=[jax.ShapeDtypeStruct(shape, dtype) for shape, dtype in outs],
        in_specs=[SMEM if a.ndim == 1 else VMEM for a in args],
        out_specs=[VMEM] * len(outs),
        scratch_shapes=[pltpu.VMEM(shape, dtype) for shape, dtype in scratch],
        compiler_params=pltpu.CompilerParams(vmem_limit_bytes=40 * 2**20),
    )(*args)


def mixing_index(e_dev):
    rel = np.zeros((e_dev, 2, 8, 3, 8, e_dev), np.int32)
    mom = np.zeros_like(rel)
    for e_out in range(e_dev):
        for tile in range(3):
            for e_in in range(e_dev):
                rel[e_out, :, :, tile, :, e_in] = (tile - 1) * e_dev + e_in - e_out + OFFSET
    for d, (j_to, to_other) in enumerate(PLACES):
        for s, (j_from, from_other) in enumerate(PLACES):
            mom[:, 0, d, :, s, :] = 2 * (j_to + j_from) + to_other - from_other
            mom[:, 1, d, :, s, :] = 2 * (j_from - j_to) + 1 - to_other - from_other
    return rel.reshape(e_dev * 16, -1), mom.reshape(e_dev * 16, -1)


def tables_kernel(moms, pos_ref, offsets_ref, phonon_ref, coupling_ref, rel_ref, mom_ref, first_ref, second_ref,
                  wide_first_ref, wide_second_ref, mix_ref, pair_ref):
    slots = coupling_ref.shape[0]
    taps = jnp.zeros((8, moms), F32)
    row = lax.broadcasted_iota(jnp.int32, (8, moms), 0)
    for s in range(2):
        for w in range(phonon_ref.shape[1]):
            hit = row == (2 * s - 1) * offsets_ref[w] + OFFSET
            taps = taps + jnp.where(hit, phonon_ref[s, w : w + 1, :], 0.0)
    taps = taps.astype(BF16).astype(F32)
    rel, mom = rel_ref[...], (mom_ref[...] * pos_ref[1]) & (moms - 1)
    table = jnp.zeros(rel.shape, F32)
    for r in range(TAPS):
        for q in range(moms):
            table = jnp.where((rel == r) & (mom == q), taps[r : r + 1, q : q + 1], table)
    outs, ins = table.shape
    tall = (lax.broadcasted_iota(jnp.int32, (outs * ROWS, outs), 0) >> 4) == lax.broadcasted_iota(
        jnp.int32, (outs * ROWS, outs), 1)
    flat = lax.broadcasted_iota(jnp.int32, (ins, ins * ROWS), 0) == (
        lax.broadcasted_iota(jnp.int32, (ins, ins * ROWS), 1) >> 4)
    half = jnp.dot(tall.astype(BF16), table.astype(BF16), preferred_element_type=F32).astype(BF16)
    full = jnp.dot(half, flat.astype(BF16), preferred_element_type=F32)
    same = (lax.broadcasted_iota(jnp.int32, full.shape, 0) & (ROWS - 1)) == (
        lax.broadcasted_iota(jnp.int32, full.shape, 1) & (ROWS - 1))
    mix_ref[...] = jnp.where(same, full, 0.0).astype(BF16)
    bonds = jnp.concatenate([coupling_ref[n] for n in range(slots)], axis=1)

    def spread(tall_ref, wide_ref):
        half = jnp.dot(tall_ref[...], bonds, precision=lax.Precision.HIGHEST, preferred_element_type=F32)
        return jnp.dot(half, wide_ref[...], precision=lax.Precision.HIGHEST, preferred_element_type=F32)

    pair_ref[...] = (spread(first_ref, wide_first_ref) * spread(second_ref, wide_second_ref)).astype(BF16)


def tables(pos, phonon, offsets, coupling, e_dev):
    slots, orbs = coupling.shape[0], coupling.shape[1]
    moms = phonon.shape[2]
    rel, mom = mixing_index(e_dev)
    pairs = np.arange(orbs * orbs)
    picks = [(index[:, None] == np.arange(orbs)).astype(np.float32) for index in (pairs // orbs, pairs % orbs)]
    wide = [np.kron(np.eye(slots, dtype=np.float32), pick.T) for pick in picks]
    return call(
        functools.partial(tables_kernel, moms),
        [((rel.shape[0] * ROWS, rel.shape[1] * ROWS), BF16), ((orbs * orbs, slots * orbs * orbs), BF16)],
        pos, offsets, phonon, coupling, *map(jnp.asarray, (rel, mom, *picks, *wide)),
    )


def cut_kernel(chunk, groups, pos_ref, green_ref, *refs):
    extra, (own_ref, give_ref, far_ref, home_ref) = refs[:-4], refs[-4:]
    e_dev, pairs, _ = green_ref.shape
    rows = e_dev * pairs

    def put(ref, at, distance):
        group = (pos_ref[0] + distance) & (groups - 1)
        start = pl.multiple_of((chunk * groups + group) * LANES, LANES)
        ref[at, 0:rows, :] = green_ref[:, :, pl.ds(start, LANES)].reshape(rows, LANES)
        for near in extra:
            ref[at, rows:, :] = near[...]

    for i, j in enumerate(NEAR):
        put(own_ref, i, pos_ref[1] * j)
        put(give_ref, i, -pos_ref[1] * j)
    put(far_ref, 0, 4)
    put(home_ref, 0, 0)


def cut(pos, green, chunk, groups, *extra):
    height = green.shape[0] * green.shape[1] + sum(x.shape[0] for x in extra)
    return call(
        functools.partial(cut_kernel, chunk, groups),
        [((n, height, LANES), BF16) for n in (len(NEAR), len(NEAR), 1, 1)],
        pos, green, *extra,
    )


def merge_kernel(own_ref, got_ref, *out_refs):
    for i, out in enumerate(out_refs):
        out[0] = own_ref[i]
        out[1] = got_ref[i]


def merge(own, got):
    return call(merge_kernel, [((2, *own.shape[1:]), BF16)] * len(NEAR), own, got)


def stack_kernel(rows, *refs):
    blocks, outs = refs[: len(NEAR) + 2], refs[len(NEAR) + 2 :]
    at = 0
    for block in blocks:
        for i in range(block.shape[0]):
            outs[0][at] = block[i, 0:rows, :]
            for out in outs[1:]:
                out[at] = block[i, rows:, :]
            at += 1


def stack(blocks, rows):
    height = blocks[0].shape[1]
    outs = [((len(PLACES), h, LANES), BF16) for h in (rows, height - rows) if h]
    return call(functools.partial(stack_kernel, rows), outs, *blocks)


def mix_kernel(e_dev, mix_ref, low_ref, own_ref, high_ref, kept_ref, other_ref):
    places, height, width = own_ref.shape
    for g in range(height // e_dev // ROWS):
        tiles = []
        for ref in (low_ref, own_ref, high_ref):
            for i in range(places):
                for e in range(e_dev):
                    tiles.append(ref[i, pl.ds((e * (height // e_dev)) + g * ROWS, ROWS), :])
        mixed = jnp.dot(mix_ref[...], jnp.concatenate(tiles, axis=0), preferred_element_type=F32)
        mixed = mixed.reshape(e_dev, 2, places, ROWS, width)
        for e in range(e_dev):
            rows = pl.ds(e * (height // e_dev) + g * ROWS, ROWS)
            kept_ref[:, rows, :] = mixed[e, 0]
            other_ref[:, rows, :] = mixed[e, 1].astype(BF16)


def mix(matrix, low, own, high, e_dev):
    return call(functools.partial(mix_kernel, e_dev), [(own.shape, F32), (own.shape, BF16)], matrix, low, own, high)


def add_kernel(kept_ref, got_ref, *out_refs):
    at = 0
    for out in out_refs:
        for i in range(out.shape[0]):
            out[i] = (kept_ref[at] + got_ref[at].astype(F32)).astype(BF16)
            at += 1


def add(kept, got):
    return call(add_kernel, [((n, *kept.shape[1:]), BF16) for n in (2, 2, 2, 1, 1)], kept, got)


def pick_kernel(*refs):
    blocks, extra, out = refs[: len(NEAR)], refs[len(NEAR) : -1], refs[-1]
    rows = blocks[0].shape[1]
    for i, block in enumerate(blocks):
        out[i * rows : (i + 1) * rows, :] = block[1]
    at = len(NEAR) * rows
    for near in extra:
        for i in range(near.shape[0]):
            out[at : at + near.shape[1], :] = near[i]
            at += near.shape[1]


def pick(blocks, *extra):
    height = len(NEAR) * blocks[0].shape[1] + sum(x.shape[0] * x.shape[1] for x in extra)
    return call(pick_kernel, [((height, LANES), BF16)], *blocks[: len(NEAR)], *extra)[0]


def couple_kernel(groups, slots, pos_ref, pair_ref, near_ref, *refs):
    fields, (out_ref, line, seen, nears) = refs[:-4], refs[-4:]
    e_dev, pairs, atoms = out_ref.shape
    rows = e_dev * pairs
    z, way = pos_ref[0], pos_ref[1]
    core = (1 - way) >> 1

    def rank(distance, parity):
        return 2 * ((z + distance) & (groups - 1)) + parity

    given = fields[len(NEAR) + 2]
    at = len(NEAR) * rows
    for i, (j, other) in enumerate(PLACES):
        nears[rank(-way * j, core + way * other)] = near_ref[i]
        nears[rank(way * j, core + way - way * other)] = given[at : at + ROWS, :]
        at += ROWS
    line[:, 0:LANES] = jnp.zeros((rows, LANES), BF16)
    line[:, atoms : atoms + LANES] = jnp.zeros((rows, LANES), BF16)
    for chunk in range(CHUNKS):
        part = fields[chunk * (len(NEAR) + 3) :]

        def put(block, distance):
            group = (z + distance) & (groups - 1)
            seen[:, pl.ds(pl.multiple_of((chunk * groups + group) * LANES, LANES), LANES)] = block

        for i, j in enumerate(NEAR):
            put(part[i][0], -way * j)
            put(part[len(NEAR) + 2][i * rows : (i + 1) * rows, :], way * j)
        put(part[len(NEAR)][0], 4)
        put(part[len(NEAR) + 1][0], 0)
    line[:, PAD : PAD + atoms] = seen[...]
    place = lax.broadcasted_iota(jnp.int32, (SPAN, LANES), 0) - lax.broadcasted_iota(jnp.int32, (SPAN, LANES), 1) - PAD

    def step(b, carry):
        start = pl.multiple_of(b * LANES, LANES)
        window = line[:, pl.ds(start, SPAN)]
        near = nears[b].astype(F32).astype(jnp.int32)
        hits = [(place == near[n : n + 1, :]).astype(BF16) for n in range(slots)]
        taken = jnp.dot(window, jnp.concatenate(hits, axis=1), preferred_element_type=F32).astype(BF16)
        columns = [
            jnp.concatenate([taken[e * pairs : (e + 1) * pairs, n * LANES : (n + 1) * LANES] for n in range(slots)], axis=0)
            for e in range(e_dev)
        ]
        total = jnp.dot(pair_ref[...], jnp.concatenate(columns, axis=1), preferred_element_type=F32)
        for e in range(e_dev):
            out_ref[e, :, pl.ds(start, LANES)] = total[:, e * LANES : (e + 1) * LANES].astype(BF16)
        return carry

    lax.fori_loop(0, atoms // LANES, step, 0, unroll=4)


def couple(pos, pair_maps, near, fields, groups, slots, shape):
    rows = shape[0] * shape[1]
    return call(
        functools.partial(couple_kernel, groups, slots),
        [(shape, BF16)],
        pos, pair_maps, near, *fields,
        scratch=[((rows, shape[2] + LANES), BF16), ((rows, shape[2]), BF16), ((2 * groups, ROWS, LANES), BF16)],
    )[0]


def swap(x):
    return lax.ppermute(x, "core", [(0, 1), (1, 0)])


def round_ring(x, j):
    groups = lax.axis_size("z")
    pairs = [(2 * z + c, 2 * ((z + (j if c == 0 else -j)) % groups) + c) for z in range(groups) for c in range(2)]
    return lax.ppermute(x, KMOM, pairs)


def exchange(blocks):
    far = round_ring(blocks[len(NEAR)], 4)
    near = [round_ring(blocks[i], j) for i, j in reversed(list(enumerate(NEAR)))]
    return [*reversed(near), far, blocks[len(NEAR) + 1]]


def body(green_blocks, phonon, offsets, neighbours, coupling):
    groups, tiles = lax.axis_size("z"), lax.axis_size("energy")
    green = green_blocks[:, 0]
    e_dev, pairs, atoms = green.shape
    rows = e_dev * pairs
    slots = neighbours.shape[1]
    core = lax.axis_index("core")
    pos = jnp.stack([lax.axis_index("z"), 1 - 2 * core])
    forward = [(i, i + 1) for i in range(tiles - 1)]
    backward = [(i + 1, i) for i in range(tiles - 1)]
    atom = lax.axis_index(KMOM) * LANES + jnp.arange(LANES, dtype=jnp.int32)
    steps = (neighbours - atom[:, None]).T.astype(BF16)
    steps = jnp.concatenate([steps, jnp.zeros((ROWS - slots, LANES), BF16)], axis=0)
    arrived = []
    for chunk, extra in ((0, ()), (1, (steps,))):
        own, give, far, home = cut(pos, green, chunk, groups, *extra)
        arrived.append(exchange([*merge(own, swap(give)), far, home]))
    matrix, pair_maps = tables(pos, phonon, offsets, coupling, e_dev)
    stacks = [stack(arrived[0], rows), stack(arrived[1], rows)]
    near = stacks[1][1]
    fields = []
    for chunk in range(CHUNKS):
        own = stacks[chunk][0]
        low, high = lax.ppermute(own, "energy", forward), lax.ppermute(own, "energy", backward)
        kept, other = mix(matrix, low, own, high, e_dev)
        back = exchange(add(kept, swap(other)))
        fields += [*back, swap(pick(back, *((near,) if chunk == 0 else ())))]
    return couple(pos, pair_maps, near, fields, groups, slots, green.shape)[:, None]


def solution(mesh):
    torus = Mesh(mesh.devices.reshape(mesh.shape["energy"], -1, 2), ("energy", *KMOM))
    placed = (P("energy", KMOM, None, None), P(), P(), P(KMOM, None), P())
    return jax.shard_map(body, mesh=torus, in_specs=placed, out_specs=P("energy", KMOM, None, None), check_vma=False)
```

```python
import functools

import jax
import jax.numpy as jnp
import numpy as np
from jax import lax
from jax.experimental import pallas as pl
from jax.experimental.pallas import tpu as pltpu
from jax.sharding import Mesh
from jax.sharding import PartitionSpec as P

OFFSET = 2
TAPS = 2 * OFFSET + 1
ROWS = 16
COST = 1
PARTS = 1
LANES = 128
SPAN = 2 * LANES
PAD = LANES // 2
KMOM = ("z", "core")
VMEM = pl.BlockSpec(memory_space=pltpu.VMEM)
SMEM = pl.BlockSpec(memory_space=pltpu.SMEM)
BF16, F32 = jnp.bfloat16, jnp.float32

NEAR = (1, 2, 3)
EARLY = ((1, 0), (1, 1), (2, 0), (2, 1), (0, 0))
PLACES = EARLY + ((3, 0), (3, 1), (4, 0))


def call(kernel, outs, *args, scratch=(), after=()):
    def run(*refs):
        kernel(*refs[: len(args)], *refs[len(args) + len(after) :])

    return pl.pallas_call(
        run,
        out_shape=[jax.ShapeDtypeStruct(shape, dtype) for shape, dtype in outs],
        in_specs=[SMEM if a.ndim == 1 else VMEM for a in args] + [pl.BlockSpec(memory_space=pl.ANY)] * len(after),
        out_specs=[VMEM] * len(outs),
        scratch_shapes=[pltpu.VMEM(shape, dtype) for shape, dtype in scratch],
        cost_estimate=pl.CostEstimate(flops=COST, bytes_accessed=1, transcendentals=0),
        compiler_params=pltpu.CompilerParams(vmem_limit_bytes=40 * 2**20),
    )(*args, *after)


def mixing_index(e_dev):
    rel = np.zeros((e_dev, 2, 8, 3, 8, e_dev), np.int32)
    mom = np.zeros_like(rel)
    for e_out in range(e_dev):
        for tile in range(3):
            for e_in in range(e_dev):
                rel[e_out, :, :, tile, :, e_in] = (tile - 1) * e_dev + e_in - e_out + OFFSET
    for d, (j_to, to_other) in enumerate(PLACES):
        for s, (j_from, from_other) in enumerate(PLACES):
            mom[:, 0, d, :, s, :] = 2 * (j_to + j_from) + to_other - from_other
            mom[:, 1, d, :, s, :] = 2 * (j_from - j_to) + 1 - to_other - from_other
    return rel.reshape(e_dev * 16, -1), mom.reshape(e_dev * 16, -1)


def tables_kernel(moms, pos_ref, offsets_ref, phonon_ref, coupling_ref, rel_ref, mom_ref, first_ref, second_ref,
                  wide_first_ref, wide_second_ref, mix_ref, pair_ref):
    slots = coupling_ref.shape[0]
    taps = jnp.zeros((8, moms), F32)
    row = lax.broadcasted_iota(jnp.int32, (8, moms), 0)
    for s in range(2):
        for w in range(phonon_ref.shape[1]):
            hit = row == (2 * s - 1) * offsets_ref[w] + OFFSET
            taps = taps + jnp.where(hit, phonon_ref[s, w : w + 1, :], 0.0)
    taps = taps.astype(BF16).astype(F32)
    rel, mom = rel_ref[...], (mom_ref[...] * pos_ref[1]) & (moms - 1)
    table = jnp.zeros(rel.shape, F32)
    for r in range(TAPS):
        for q in range(moms):
            table = jnp.where((rel == r) & (mom == q), taps[r : r + 1, q : q + 1], table)
    outs, ins = table.shape
    tall = (lax.broadcasted_iota(jnp.int32, (outs * ROWS, outs), 0) >> 4) == lax.broadcasted_iota(
        jnp.int32, (outs * ROWS, outs), 1)
    flat = lax.broadcasted_iota(jnp.int32, (ins, ins * ROWS), 0) == (
        lax.broadcasted_iota(jnp.int32, (ins, ins * ROWS), 1) >> 4)
    half = jnp.dot(tall.astype(BF16), table.astype(BF16), preferred_element_type=F32).astype(BF16)
    full = jnp.dot(half, flat.astype(BF16), preferred_element_type=F32)
    same = (lax.broadcasted_iota(jnp.int32, full.shape, 0) & (ROWS - 1)) == (
        lax.broadcasted_iota(jnp.int32, full.shape, 1) & (ROWS - 1))
    mix_ref[...] = jnp.where(same, full, 0.0).astype(BF16)
    bonds = jnp.concatenate([coupling_ref[n] for n in range(slots)], axis=1)

    def spread(tall_ref, wide_ref):
        half = jnp.dot(tall_ref[...], bonds, precision=lax.Precision.HIGHEST, preferred_element_type=F32)
        return jnp.dot(half, wide_ref[...], precision=lax.Precision.HIGHEST, preferred_element_type=F32)

    pair_ref[...] = (spread(first_ref, wide_first_ref) * spread(second_ref, wide_second_ref)).astype(BF16)


def tables(pos, phonon, offsets, coupling, e_dev):
    slots, orbs = coupling.shape[0], coupling.shape[1]
    moms = phonon.shape[2]
    rel, mom = mixing_index(e_dev)
    pairs = np.arange(orbs * orbs)
    picks = [(index[:, None] == np.arange(orbs)).astype(np.float32) for index in (pairs // orbs, pairs % orbs)]
    wide = [np.kron(np.eye(slots, dtype=np.float32), pick.T) for pick in picks]
    return call(
        functools.partial(tables_kernel, moms),
        [((rel.shape[0] * ROWS, rel.shape[1] * ROWS), BF16), ((orbs * orbs, slots * orbs * orbs), BF16)],
        pos, offsets, phonon, coupling, *map(jnp.asarray, (rel, mom, *picks, *wide)),
    )


def cut_kernel(groups, pos_ref, green_ref, near_ref, own_ref, give_ref, far_ref, home_ref):
    e_dev, pairs, _ = green_ref.shape
    rows = e_dev * pairs

    def put(ref, at, distance):
        group = (pos_ref[0] + distance) & (groups - 1)
        for chunk in range(2):
            start = pl.multiple_of((chunk * groups + group) * LANES, LANES)
            ref[at, chunk * rows : (chunk + 1) * rows, :] = green_ref[:, :, pl.ds(start, LANES)].reshape(rows, LANES)
        ref[at, 2 * rows :, :] = near_ref[...]

    for i, j in enumerate(NEAR):
        put(own_ref, i, pos_ref[1] * j)
        put(give_ref, i, -pos_ref[1] * j)
    put(far_ref, 0, 4)
    put(home_ref, 0, 0)


def cut(pos, green, near, groups):
    height = 2 * green.shape[0] * green.shape[1] + near.shape[0]
    outs = [((n, height, LANES), BF16) for n in (len(NEAR), len(NEAR), 1, 1)]
    return call(functools.partial(cut_kernel, groups), outs, pos, green, near)


def merge_kernel(chips, own_ref, got_ref, *refs):
    whole = refs[: len(refs) - len(chips) >> 1]
    outs = refs[len(whole) :]
    for out, j in zip(outs, chips):
        out[0] = own_ref[j - 1]
        out[1] = got_ref[j - 1]
    for out, ref in zip(outs[len(chips) :], whole):
        out[...] = ref[...]


def merge(own, got, chips, *whole, after=()):
    outs = [((2, *own.shape[1:]), BF16)] * len(chips) + [(x.shape, BF16) for x in whole]
    return call(functools.partial(merge_kernel, chips), outs, own, got, *whole, after=after)


def stack_kernel(*refs):
    blocks, (out_ref, near_ref) = refs[:-2], refs[-2:]
    rows = out_ref.shape[1]
    at = 0
    for block in blocks:
        for i in range(block.shape[0]):
            out_ref[at] = block[i, 0:rows, :]
            near_ref[at] = block[i, rows:, :]
            at += 1


def stack(*blocks):
    places = sum(b.shape[0] for b in blocks)
    outs = [((places, h, LANES), BF16) for h in (blocks[0].shape[1] - ROWS, ROWS)]
    return call(stack_kernel, outs, *blocks)


def mix_kernel(e_dev, chunk, mix_ref, *refs):
    fields, kept_ref, other_ref = refs[:6], refs[6], refs[7]
    places, height, width = kept_ref.shape
    pairs = height // e_dev
    for g in range(pairs // ROWS):
        tiles = []
        for ref in fields:
            for i in range(ref.shape[0]):
                for e in range(e_dev):
                    tiles.append(ref[i, pl.ds(chunk * height + e * pairs + g * ROWS, ROWS), :])
        mixed = jnp.dot(mix_ref[...], jnp.concatenate(tiles, axis=0), preferred_element_type=F32)
        mixed = mixed.reshape(e_dev, 2, places, ROWS, width)
        for e in range(e_dev):
            rows = pl.ds(e * pairs + g * ROWS, ROWS)
            kept_ref[:, rows, :] = mixed[e, 0]
            other_ref[:, rows, :] = mixed[e, 1].astype(BF16)


def mix(matrix, fields, chunk, e_dev, after=()):
    shape = (len(PLACES), fields[0].shape[1] // 2, LANES)
    return call(functools.partial(mix_kernel, e_dev, chunk), [(shape, F32), (shape, BF16)], matrix, *fields, after=after)


def add_kernel(kept_ref, got_ref, far, three, two, one, home):
    at = 0
    for out in (one, two, home, three, far):
        for i in range(out.shape[0]):
            out[i] = (kept_ref[at] + got_ref[at].astype(F32)).astype(BF16)
            at += 1


def add(kept, got, after=()):
    return call(add_kernel, [((n, *kept.shape[1:]), BF16) for n in (1, 2, 2, 2, 1)], kept, got, after=after)


def pick_kernel(*refs):
    blocks, extra, out = refs[: len(NEAR)], refs[len(NEAR) : -1], refs[-1]
    rows = blocks[0].shape[1]
    for i, block in enumerate(blocks):
        out[i * rows : (i + 1) * rows, :] = block[1]
    at = len(NEAR) * rows
    for near in extra:
        for i in range(near.shape[0]):
            out[at : at + near.shape[1], :] = near[i]
            at += near.shape[1]


def pick(blocks, *extra, after=()):
    height = len(NEAR) * blocks[1].shape[1] + sum(x.shape[0] * x.shape[1] for x in extra)
    return call(pick_kernel, [((height, LANES), BF16)], *blocks[3:0:-1], *extra, after=(blocks[0], *after))[0]


def gather_line(pos_ref, groups, line, base, far_ref, three_ref, two_ref, one_ref, home_ref, given_ref):
    z, way = pos_ref[0], pos_ref[1]
    rows = far_ref.shape[1]

    def put(block, distance):
        group = (z + distance) & (groups - 1)
        line[:, pl.ds(pl.multiple_of(base + group * LANES, LANES), LANES)] = block

    for i, (j, ref) in enumerate(zip(NEAR, (one_ref, two_ref, three_ref))):
        put(ref[0], -way * j)
        put(given_ref[i * rows : (i + 1) * rows, :], way * j)
    put(far_ref[0], 4)
    put(home_ref[0], 0)


def sum_block(line, window_at, near, pair_ref, e_dev):
    slots, pairs = pair_ref.shape[1] // pair_ref.shape[0], pair_ref.shape[0]
    place = lax.broadcasted_iota(jnp.int32, (SPAN, LANES), 0) - lax.broadcasted_iota(jnp.int32, (SPAN, LANES), 1) - PAD
    near = near.astype(F32).astype(jnp.int32)
    hits = [(place == near[n : n + 1, :]).astype(BF16) for n in range(slots)]
    window = line[:, pl.ds(window_at, SPAN)]
    taken = jnp.dot(window, jnp.concatenate(hits, axis=1), preferred_element_type=F32).astype(BF16)
    columns = [
        jnp.concatenate([taken[e * pairs : (e + 1) * pairs, n * LANES : (n + 1) * LANES] for n in range(slots)], axis=0)
        for e in range(e_dev)
    ]
    return jnp.dot(pair_ref[...], jnp.concatenate(columns, axis=1), preferred_element_type=F32).astype(BF16)


def first_kernel(groups, pos_ref, pair_ref, early_ref, late_ref, *refs):
    blocks, (out_ref, nears, tail, line, seen) = refs[:6], refs[6:]
    e_dev, pairs, atoms = out_ref.shape
    rows = e_dev * pairs
    z, way = pos_ref[0], pos_ref[1]
    core = (1 - way) >> 1

    def rank(distance, parity):
        return 2 * ((z + distance) & (groups - 1)) + parity

    at = len(NEAR) * rows
    for i, (j, other) in enumerate(PLACES):
        nears[rank(-way * j, core + way * other)] = early_ref[i] if i < len(EARLY) else late_ref[i - len(EARLY)]
        nears[rank(way * j, core + way - way * other)] = blocks[5][at : at + ROWS, :]
        at += ROWS
    gather_line(pos_ref, groups, seen, 0, *blocks)
    tail[...] = seen[:, groups * LANES - LANES - PAD :]
    line[:, 0:LANES] = jnp.zeros((rows, LANES), BF16)
    line[:, PAD : PAD + groups * LANES] = seen[...]

    def step(b, carry):
        start = pl.multiple_of(b * LANES, LANES)
        total = sum_block(line, start, nears[b], pair_ref, e_dev)
        for e in range(e_dev):
            out_ref[e, :, pl.ds(start, LANES)] = total[:, e * LANES : (e + 1) * LANES]
        return carry

    lax.fori_loop(0, atoms // LANES, step, 0, unroll=True)


def first_sum(pos, pair_maps, nears, blocks, groups, shape):
    rows = shape[0] * shape[1]
    return call(
        functools.partial(first_kernel, groups),
        [((*shape[:2], (groups - 1) * LANES), BF16), ((2 * groups, ROWS, LANES), BF16), ((rows, LANES + PAD), BF16)],
        pos, pair_maps, *nears, *blocks,
        scratch=[((rows, groups * LANES + LANES), BF16), ((rows, groups * LANES), BF16)],
    )


def second_kernel(groups, pos_ref, pair_ref, nears, done_ref, tail_ref, *refs):
    blocks, (out_ref, line, seen) = refs[:6], refs[6:]
    e_dev, pairs, atoms = out_ref.shape
    rows = e_dev * pairs
    first = done_ref.shape[2] // LANES
    width = (groups + 1) * LANES
    out_ref[:, :, 0 : first * LANES] = done_ref[...]
    gather_line(pos_ref, groups, seen, 0, *blocks)
    line[:, width:] = jnp.zeros((rows, LANES), BF16)
    line[:, 0 : LANES + PAD] = tail_ref[...]
    line[:, LANES + PAD : PAD + width] = seen[...]

    def step(b, carry):
        start = pl.multiple_of(b * LANES, LANES)
        total = sum_block(line, start, nears[b + first], pair_ref, e_dev)
        for e in range(e_dev):
            out_ref[e, :, pl.ds(pl.multiple_of(start + first * LANES, LANES), LANES)] = total[:, e * LANES : (e + 1) * LANES]
        return carry

    lax.fori_loop(0, atoms // LANES - first, step, 0, unroll=True)


def second_sum(pos, pair_maps, nears, done, tail, blocks, groups, shape):
    rows = shape[0] * shape[1]
    return call(
        functools.partial(second_kernel, groups),
        [(shape, BF16)],
        pos, pair_maps, nears, done, tail, *blocks,
        scratch=[((rows, (groups + 2) * LANES), BF16), ((rows, groups * LANES), BF16)],
    )[0]


def swap(x):
    return lax.ppermute(x, "core", [(0, 1), (1, 0)])


def round_ring(x, j):
    groups = lax.axis_size("z")
    pairs = [(2 * z + c, 2 * ((z + (j if c == 0 else -j)) % groups) + c) for z in range(groups) for c in range(2)]
    return lax.ppermute(x, KMOM, pairs)


def exchange(far, three, two, one, home):
    return [round_ring(far, 4), round_ring(three, 3), round_ring(two, 2), round_ring(one, 1), home]


def body(green_blocks, phonon, offsets, neighbours, coupling):
    groups, tiles = lax.axis_size("z"), lax.axis_size("energy")
    green = green_blocks[:, 0]
    e_dev, pairs, atoms = green.shape
    rows = e_dev * pairs
    slots = neighbours.shape[1]
    core = lax.axis_index("core")
    pos = jnp.stack([lax.axis_index("z"), 1 - 2 * core])
    forward = [(i, i + 1) for i in range(tiles - 1)]
    backward = [(i + 1, i) for i in range(tiles - 1)]
    atom = lax.axis_index(KMOM) * LANES + jnp.arange(LANES, dtype=jnp.int32)
    steps = (neighbours - atom[:, None]).T.astype(BF16)
    steps = jnp.concatenate([steps, jnp.zeros((ROWS - slots, LANES), BF16)], axis=0)

    own, give, far, home = cut(pos, green, steps, groups)
    far, three, two, one, home = exchange(far, *merge(own, swap(give), (3, 2, 1)), home)
    parts = [stack(one, two, home), stack(three, far)]
    fields, near = zip(*parts)
    low = [lax.ppermute(x, "energy", forward) for x in fields]
    high = [lax.ppermute(x, "energy", backward) for x in fields]
    fields = (*low, *fields, *high)
    matrix, pair_maps = tables(pos, phonon, offsets, coupling, e_dev)
    backs = []
    for chunk in range(2):
        kept, other = mix(matrix, fields, chunk, e_dev)
        backs.append(exchange(*add(kept, swap(other))))
    blocks = [*backs[0], swap(pick(backs[0], *near))]
    done, nears, tail = first_sum(pos, pair_maps, near, blocks, groups, green.shape)
    blocks = [*backs[1], swap(pick(backs[1]))]
    return second_sum(pos, pair_maps, nears, done, tail, blocks, groups, green.shape)[:, None]


def solution(mesh):
    torus = Mesh(mesh.devices.reshape(mesh.shape["energy"], -1, 2), ("energy", *KMOM))
    placed = (P("energy", KMOM, None, None), P(), P(), P(KMOM, None), P())
    return jax.shard_map(body, mesh=torus, in_specs=placed, out_specs=P("energy", KMOM, None, None), check_vma=False)
```

```python
import functools

import jax
import jax.numpy as jnp
import numpy as np
from jax import lax
from jax.experimental import pallas as pl
from jax.experimental.pallas import tpu as pltpu
from jax.sharding import Mesh
from jax.sharding import PartitionSpec as P

OFFSET = 2
TAPS = 2 * OFFSET + 1
ROWS = 16
COST = 1
PARTS = 1
LANES = 128
SPAN = 2 * LANES
PAD = LANES // 2
KMOM = ("z", "core")
VMEM = pl.BlockSpec(memory_space=pltpu.VMEM)
SMEM = pl.BlockSpec(memory_space=pltpu.SMEM)
BF16, F32 = jnp.bfloat16, jnp.float32

NEAR = (1, 2, 3)
EARLY = ((1, 0), (1, 1), (2, 0), (2, 1), (0, 0))
LATE = ((3, 0), (3, 1), (4, 0))
PLACES = EARLY + LATE
SEEN = ((-1, EARLY), (0, EARLY), (1, EARLY), (0, LATE))
LAST = ((-1, LATE), (1, LATE))


def call(kernel, outs, *args, scratch=(), after=()):
    def run(*refs):
        kernel(*refs[: len(args)], *refs[len(args) + len(after) :])

    return pl.pallas_call(
        run,
        out_shape=[jax.ShapeDtypeStruct(shape, dtype) for shape, dtype in outs],
        in_specs=[SMEM if a.ndim == 1 else VMEM for a in args] + [pl.BlockSpec(memory_space=pl.ANY)] * len(after),
        out_specs=[VMEM] * len(outs),
        scratch_shapes=[pltpu.VMEM(shape, dtype) for shape, dtype in scratch],
        cost_estimate=pl.CostEstimate(flops=COST, bytes_accessed=1, transcendentals=0),
        compiler_params=pltpu.CompilerParams(vmem_limit_bytes=40 * 2**20),
    )(*args, *after)


def mixing_index(e_dev):
    columns = [(tile, place, e) for parts in (SEEN, LAST) for tile, part in parts for place in part for e in range(e_dev)]
    rel = np.zeros((e_dev, 2, len(PLACES), len(columns)), np.int32)
    mom = np.zeros_like(rel)
    for at, (tile, (j_from, from_other), e_in) in enumerate(columns):
        for e_out in range(e_dev):
            rel[e_out, ..., at] = tile * e_dev + e_in - e_out + OFFSET
        for d, (j_to, to_other) in enumerate(PLACES):
            mom[:, 0, d, at] = 2 * (j_to + j_from) + to_other - from_other
            mom[:, 1, d, at] = 2 * (j_from - j_to) + 1 - to_other - from_other
    return rel.reshape(-1, len(columns)), mom.reshape(-1, len(columns))


def tables_kernel(moms, pos_ref, offsets_ref, phonon_ref, coupling_ref, rel_ref, mom_ref, first_ref, second_ref,
                  wide_first_ref, wide_second_ref, seen_ref, last_ref, pair_ref):
    slots = coupling_ref.shape[0]
    taps = jnp.zeros((8, moms), F32)
    row = lax.broadcasted_iota(jnp.int32, (8, moms), 0)
    for s in range(2):
        for w in range(phonon_ref.shape[1]):
            hit = row == (2 * s - 1) * offsets_ref[w] + OFFSET
            taps = taps + jnp.where(hit, phonon_ref[s, w : w + 1, :], 0.0)
    taps = taps.astype(BF16).astype(F32)
    rel, mom = rel_ref[...], (mom_ref[...] * pos_ref[1]) & (moms - 1)
    table = jnp.zeros(rel.shape, F32)
    for r in range(TAPS):
        for q in range(moms):
            table = jnp.where((rel == r) & (mom == q), taps[r : r + 1, q : q + 1], table)
    outs, ins = table.shape
    tall = (lax.broadcasted_iota(jnp.int32, (outs * ROWS, outs), 0) >> 4) == lax.broadcasted_iota(
        jnp.int32, (outs * ROWS, outs), 1)
    half = jnp.dot(tall.astype(BF16), table.astype(BF16), preferred_element_type=F32).astype(BF16)
    start = 0
    for ref in (seen_ref, last_ref):
        height, width = ref.shape
        flat = lax.broadcasted_iota(jnp.int32, (ins, width), 0) == (
            (lax.broadcasted_iota(jnp.int32, (ins, width), 1) + start) >> 4)
        full = jnp.dot(half, flat.astype(BF16), preferred_element_type=F32)
        same = (lax.broadcasted_iota(jnp.int32, ref.shape, 0) & (ROWS - 1)) == (
            lax.broadcasted_iota(jnp.int32, ref.shape, 1) & (ROWS - 1))
        ref[...] = jnp.where(same, full, 0.0).astype(BF16)
        start += width
    bonds = jnp.concatenate([coupling_ref[n] for n in range(slots)], axis=1)

    def spread(tall_ref, wide_ref):
        half = jnp.dot(tall_ref[...], bonds, precision=lax.Precision.HIGHEST, preferred_element_type=F32)
        return jnp.dot(half, wide_ref[...], precision=lax.Precision.HIGHEST, preferred_element_type=F32)

    pair_ref[...] = (spread(first_ref, wide_first_ref) * spread(second_ref, wide_second_ref)).astype(BF16)


def tables(pos, phonon, offsets, coupling, e_dev):
    slots, orbs = coupling.shape[0], coupling.shape[1]
    moms = phonon.shape[2]
    rel, mom = mixing_index(e_dev)
    pairs = np.arange(orbs * orbs)
    picks = [(index[:, None] == np.arange(orbs)).astype(np.float32) for index in (pairs // orbs, pairs % orbs)]
    wide = [np.kron(np.eye(slots, dtype=np.float32), pick.T) for pick in picks]
    return call(
        functools.partial(tables_kernel, moms),
        [((rel.shape[0] * ROWS, n * e_dev * ROWS), BF16) for n in (sum(len(p) for _, p in x) for x in (SEEN, LAST))]
        + [((orbs * orbs, slots * orbs * orbs), BF16)],
        pos, offsets, phonon, coupling, *map(jnp.asarray, (rel, mom, *picks, *wide)),
    )


def cut_kernel(groups, pos_ref, near_ref, green_ref, own_ref, give_ref, far_ref, home_ref):
    e_dev, pairs, _ = green_ref.shape
    rows = e_dev * pairs
    z, way = pos_ref[0], pos_ref[1]
    first = (2 * z + ((1 - way) >> 1)) * LANES
    steps = (near_ref[...] - first - lax.broadcasted_iota(jnp.int32, near_ref.shape, 1)).astype(F32)
    steps = jnp.concatenate([steps, jnp.zeros((ROWS - steps.shape[0], LANES), F32)], axis=0).astype(BF16)

    def put(ref, at, distance):
        group = (z + distance) & (groups - 1)
        for chunk in range(2):
            start = pl.multiple_of((chunk * groups + group) * LANES, LANES)
            ref[at, chunk * rows : (chunk + 1) * rows, :] = green_ref[:, :, pl.ds(start, LANES)].reshape(rows, LANES)
        ref[at, 2 * rows :, :] = steps

    for i, j in enumerate(NEAR):
        put(own_ref, i, way * j)
        put(give_ref, i, -way * j)
    put(far_ref, 0, 4)
    put(home_ref, 0, 0)


def cut(pos, near, green, groups):
    height = 2 * green.shape[0] * green.shape[1] + ROWS
    outs = [((n, height, LANES), BF16) for n in (len(NEAR), len(NEAR), 1, 1)]
    return call(functools.partial(cut_kernel, groups), outs, pos, near, green)


def merge_kernel(chips, own_ref, got_ref, *refs):
    whole = refs[: len(refs) - len(chips) >> 1]
    outs = refs[len(whole) :]
    for out, j in zip(outs, chips):
        out[0] = own_ref[j - 1]
        out[1] = got_ref[j - 1]
    for out, ref in zip(outs[len(chips) :], whole):
        out[...] = ref[...]


def merge(own, got, chips, *whole, after=()):
    outs = [((2, *own.shape[1:]), BF16)] * len(chips) + [(x.shape, BF16) for x in whole]
    return call(functools.partial(merge_kernel, chips), outs, own, got, *whole, after=after)


def stack_kernel(*refs):
    blocks, (out_ref, near_ref) = refs[:-2], refs[-2:]
    rows = out_ref.shape[1]
    at = 0
    for block in blocks:
        for i in range(block.shape[0]):
            out_ref[at] = block[i, 0:rows, :]
            near_ref[at] = block[i, rows:, :]
            at += 1


def stack(*blocks):
    places = sum(b.shape[0] for b in blocks)
    outs = [((places, h, LANES), BF16) for h in (blocks[0].shape[1] - ROWS, ROWS)]
    return call(stack_kernel, outs, *blocks)


def mix_kernel(e_dev, chunk, fields, mix_ref, *refs):
    refs, sums, (kept_ref, other_ref) = refs[:fields], refs[fields:-2], refs[-2:]
    places, height, width = kept_ref.shape
    pairs = height // e_dev
    for g in range(pairs // ROWS):
        tiles = []
        for ref in refs:
            for i in range(ref.shape[0]):
                for e in range(e_dev):
                    tiles.append(ref[i, pl.ds(chunk * height + e * pairs + g * ROWS, ROWS), :])
        mixed = jnp.dot(mix_ref[...], jnp.concatenate(tiles, axis=0), preferred_element_type=F32)
        mixed = mixed.reshape(e_dev, 2, places, ROWS, width)
        for e in range(e_dev):
            rows = pl.ds(e * pairs + g * ROWS, ROWS)
            for i, out in enumerate((kept_ref, other_ref)):
                total = mixed[e, i] + sums[i][:, rows, :] if sums else mixed[e, i]
                out[:, rows, :] = total.astype(out.dtype)


def mix(matrix, fields, chunk, e_dev, sums=(), after=()):
    shape = (len(PLACES), fields[0].shape[1] // 2, LANES)
    outs = [(shape, F32), (shape, BF16 if sums else F32)]
    return call(functools.partial(mix_kernel, e_dev, chunk, len(fields)), outs, matrix, *fields, *sums, after=after)


def add_kernel(kept_ref, got_ref, far, three, two, one, home):
    at = 0
    for out in (one, two, home, three, far):
        for i in range(out.shape[0]):
            out[i] = (kept_ref[at] + got_ref[at].astype(F32)).astype(BF16)
            at += 1


def add(kept, got, after=()):
    return call(add_kernel, [((n, *kept.shape[1:]), BF16) for n in (1, 2, 2, 2, 1)], kept, got, after=after)


def pick_kernel(*refs):
    blocks, extra, out = refs[: len(NEAR)], refs[len(NEAR) : -1], refs[-1]
    rows = blocks[0].shape[1]
    for i, block in enumerate(blocks):
        out[i * rows : (i + 1) * rows, :] = block[1]
    at = len(NEAR) * rows
    for near in extra:
        for i in range(near.shape[0]):
            out[at : at + near.shape[1], :] = near[i]
            at += near.shape[1]


def pick(blocks, *extra, after=()):
    height = len(NEAR) * blocks[1].shape[1] + sum(x.shape[0] * x.shape[1] for x in extra)
    return call(pick_kernel, [((height, LANES), BF16)], *blocks[3:0:-1], *extra, after=(blocks[0], *after))[0]


def gather_line(pos_ref, groups, line, base, far_ref, three_ref, two_ref, one_ref, home_ref, given_ref):
    z, way = pos_ref[0], pos_ref[1]
    rows = far_ref.shape[1]

    def put(block, distance):
        group = (z + distance) & (groups - 1)
        line[:, pl.ds(pl.multiple_of(base + group * LANES, LANES), LANES)] = block

    for i, (j, ref) in enumerate(zip(NEAR, (one_ref, two_ref, three_ref))):
        put(ref[0], -way * j)
        put(given_ref[i * rows : (i + 1) * rows, :], way * j)
    put(far_ref[0], 4)
    put(home_ref[0], 0)


def sum_block(line, window_at, near, pair_ref, e_dev):
    slots, pairs = pair_ref.shape[1] // pair_ref.shape[0], pair_ref.shape[0]
    place = lax.broadcasted_iota(jnp.int32, (SPAN, LANES), 0) - lax.broadcasted_iota(jnp.int32, (SPAN, LANES), 1) - PAD
    near = near.astype(F32).astype(jnp.int32)
    hits = [(place == near[n : n + 1, :]).astype(BF16) for n in range(slots)]
    window = line[:, pl.ds(window_at, SPAN)]
    taken = jnp.dot(window, jnp.concatenate(hits, axis=1), preferred_element_type=F32).astype(BF16)
    columns = [
        jnp.concatenate([taken[e * pairs : (e + 1) * pairs, n * LANES : (n + 1) * LANES] for n in range(slots)], axis=0)
        for e in range(e_dev)
    ]
    return jnp.dot(pair_ref[...], jnp.concatenate(columns, axis=1), preferred_element_type=F32).astype(BF16)


def first_kernel(groups, pos_ref, pair_ref, early_ref, late_ref, *refs):
    blocks, (out_ref, nears, tail, line, seen) = refs[:6], refs[6:]
    e_dev, pairs, atoms = out_ref.shape
    rows = e_dev * pairs
    z, way = pos_ref[0], pos_ref[1]
    core = (1 - way) >> 1

    def rank(distance, parity):
        return 2 * ((z + distance) & (groups - 1)) + parity

    at = len(NEAR) * rows
    for i, (j, other) in enumerate(PLACES):
        nears[rank(-way * j, core + way * other)] = early_ref[i] if i < len(EARLY) else late_ref[i - len(EARLY)]
        nears[rank(way * j, core + way - way * other)] = blocks[5][at : at + ROWS, :]
        at += ROWS
    gather_line(pos_ref, groups, seen, 0, *blocks)
    tail[...] = seen[:, groups * LANES - LANES - PAD :]
    line[:, 0:LANES] = jnp.zeros((rows, LANES), BF16)
    line[:, PAD : PAD + groups * LANES] = seen[...]

    def step(b, carry):
        start = pl.multiple_of(b * LANES, LANES)
        total = sum_block(line, start, nears[b], pair_ref, e_dev)
        for e in range(e_dev):
            out_ref[e, :, pl.ds(start, LANES)] = total[:, e * LANES : (e + 1) * LANES]
        return carry

    lax.fori_loop(0, atoms // LANES, step, 0, unroll=True)


def first_sum(pos, pair_maps, nears, blocks, groups, shape):
    rows = shape[0] * shape[1]
    return call(
        functools.partial(first_kernel, groups),
        [((*shape[:2], (groups - 1) * LANES), BF16), ((2 * groups, ROWS, LANES), BF16), ((rows, LANES + PAD), BF16)],
        pos, pair_maps, *nears, *blocks,
        scratch=[((rows, groups * LANES + LANES), BF16), ((rows, groups * LANES), BF16)],
    )


def second_kernel(groups, pos_ref, pair_ref, nears, done_ref, tail_ref, *refs):
    blocks, (out_ref, line, seen) = refs[:6], refs[6:]
    e_dev, pairs, atoms = out_ref.shape
    rows = e_dev * pairs
    first = done_ref.shape[2] // LANES
    width = (groups + 1) * LANES
    out_ref[:, :, 0 : first * LANES] = done_ref[...]
    gather_line(pos_ref, groups, seen, 0, *blocks)
    line[:, width:] = jnp.zeros((rows, LANES), BF16)
    line[:, 0 : LANES + PAD] = tail_ref[...]
    line[:, LANES + PAD : PAD + width] = seen[...]

    def step(b, carry):
        start = pl.multiple_of(b * LANES, LANES)
        total = sum_block(line, start, nears[b + first], pair_ref, e_dev)
        for e in range(e_dev):
            out_ref[e, :, pl.ds(pl.multiple_of(start + first * LANES, LANES), LANES)] = total[:, e * LANES : (e + 1) * LANES]
        return carry

    lax.fori_loop(0, atoms // LANES - first, step, 0, unroll=True)


def second_sum(pos, pair_maps, nears, done, tail, blocks, groups, shape):
    rows = shape[0] * shape[1]
    return call(
        functools.partial(second_kernel, groups),
        [(shape, BF16)],
        pos, pair_maps, nears, done, tail, *blocks,
        scratch=[((rows, (groups + 2) * LANES), BF16), ((rows, groups * LANES), BF16)],
    )[0]


def swap(x):
    return lax.ppermute(x, "core", [(0, 1), (1, 0)])


def round_ring(x, j):
    groups = lax.axis_size("z")
    pairs = [(2 * z + c, 2 * ((z + (j if c == 0 else -j)) % groups) + c) for z in range(groups) for c in range(2)]
    return lax.ppermute(x, KMOM, pairs)


def exchange(far, three, two, one, home):
    return [round_ring(far, 4), round_ring(three, 3), round_ring(two, 2), round_ring(one, 1), home]


def body(green_blocks, phonon, offsets, neighbours, coupling):
    groups, tiles = lax.axis_size("z"), lax.axis_size("energy")
    green = green_blocks[:, 0]
    e_dev, pairs, atoms = green.shape
    rows = e_dev * pairs
    core = lax.axis_index("core")
    pos = jnp.stack([lax.axis_index("z"), 1 - 2 * core])
    forward = [(i, i + 1) for i in range(tiles - 1)]
    backward = [(i + 1, i) for i in range(tiles - 1)]
    own, give, far, home = cut(pos, neighbours.T, green, groups)
    far, three, two, one, home = exchange(far, *merge(own, swap(give), (3, 2, 1)), home)
    parts = [stack(one, two, home), stack(three, far)]
    fields, near = zip(*parts)
    low = [lax.ppermute(x, "energy", forward) for x in fields]
    high = [lax.ppermute(x, "energy", backward) for x in fields]
    seen, last, pair_maps = tables(pos, phonon, offsets, coupling, e_dev)
    sums = [mix(seen, (low[0], fields[0], high[0], fields[1]), chunk, e_dev) for chunk in range(2)]
    backs = []
    for chunk in range(2):
        kept, other = mix(last, (low[1], high[1]), chunk, e_dev, sums[chunk], after=sums[1][:1])
        backs.append(exchange(*add(kept, swap(other))))
    blocks = [*backs[0], swap(pick(backs[0], *near))]
    done, nears, tail = first_sum(pos, pair_maps, near, blocks, groups, green.shape)
    blocks = [*backs[1], swap(pick(backs[1]))]
    return second_sum(pos, pair_maps, nears, done, tail, blocks, groups, green.shape)[:, None]


def solution(mesh):
    torus = Mesh(mesh.devices.reshape(mesh.shape["energy"], -1, 2), ("energy", *KMOM))
    placed = (P("energy", KMOM, None, None), P(), P(), P(KMOM, None), P())
    return jax.shard_map(body, mesh=torus, in_specs=placed, out_specs=P("energy", KMOM, None, None), check_vma=False)
```

```python
import functools

import jax
import jax.numpy as jnp
import numpy as np
from jax import lax
from jax.experimental import pallas as pl
from jax.experimental.pallas import tpu as pltpu
from jax.sharding import Mesh
from jax.sharding import PartitionSpec as P

OFFSET = 2
TAPS = 2 * OFFSET + 1
ROWS = 16
COST = 1
TABLES = 20000000000
PARTS = 1
LANES = 128
SPAN = 2 * LANES
PAD = LANES // 2
KMOM = ("z", "core")
VMEM = pl.BlockSpec(memory_space=pltpu.VMEM)
SMEM = pl.BlockSpec(memory_space=pltpu.SMEM)
BF16, F32 = jnp.bfloat16, jnp.float32

NEAR = (1, 2, 3)
EARLY = ((1, 0), (1, 1), (2, 0), (2, 1), (0, 0))
LATE = ((3, 0), (3, 1), (4, 0))
PLACES = EARLY + LATE
SEEN = ((-1, EARLY), (0, EARLY), (1, EARLY), (0, LATE))
LAST = ((-1, LATE), (1, LATE))


def call(kernel, outs, *args, scratch=(), after=(), cost=COST):
    def run(*refs):
        kernel(*refs[: len(args)], *refs[len(args) + len(after) :])

    return pl.pallas_call(
        run,
        out_shape=[jax.ShapeDtypeStruct(shape, dtype) for shape, dtype in outs],
        in_specs=[SMEM if a.ndim == 1 else VMEM for a in args] + [pl.BlockSpec(memory_space=pl.ANY)] * len(after),
        out_specs=[VMEM] * len(outs),
        scratch_shapes=[pltpu.VMEM(shape, dtype) for shape, dtype in scratch],
        cost_estimate=pl.CostEstimate(flops=cost, bytes_accessed=1, transcendentals=0),
        compiler_params=pltpu.CompilerParams(vmem_limit_bytes=40 * 2**20),
    )(*args, *after)


def mixing_index(e_dev):
    columns = [(tile, place, e) for parts in (SEEN, LAST) for tile, part in parts for place in part for e in range(e_dev)]
    rel = np.zeros((e_dev, 2, len(PLACES), len(columns)), np.int32)
    mom = np.zeros_like(rel)
    for at, (tile, (j_from, from_other), e_in) in enumerate(columns):
        for e_out in range(e_dev):
            rel[e_out, ..., at] = tile * e_dev + e_in - e_out + OFFSET
        for d, (j_to, to_other) in enumerate(PLACES):
            mom[:, 0, d, at] = 2 * (j_to + j_from) + to_other - from_other
            mom[:, 1, d, at] = 2 * (j_from - j_to) + 1 - to_other - from_other
    return rel.reshape(-1, len(columns)), mom.reshape(-1, len(columns))


def tables_kernel(moms, pos_ref, offsets_ref, phonon_ref, coupling_ref, rel_ref, mom_ref, first_ref, second_ref,
                  wide_first_ref, wide_second_ref, seen_ref, last_ref, pair_ref):
    slots = coupling_ref.shape[0]
    taps = jnp.zeros((8, moms), F32)
    row = lax.broadcasted_iota(jnp.int32, (8, moms), 0)
    for s in range(2):
        for w in range(phonon_ref.shape[1]):
            hit = row == (2 * s - 1) * offsets_ref[w] + OFFSET
            taps = taps + jnp.where(hit, phonon_ref[s, w : w + 1, :], 0.0)
    taps = taps.astype(BF16).astype(F32)
    rel, mom = rel_ref[...], (mom_ref[...] * pos_ref[1]) & (moms - 1)
    table = jnp.zeros(rel.shape, F32)
    for r in range(TAPS):
        for q in range(moms):
            table = jnp.where((rel == r) & (mom == q), taps[r : r + 1, q : q + 1], table)
    outs, ins = table.shape
    tall = (lax.broadcasted_iota(jnp.int32, (outs * ROWS, outs), 0) >> 4) == lax.broadcasted_iota(
        jnp.int32, (outs * ROWS, outs), 1)
    half = jnp.dot(tall.astype(BF16), table.astype(BF16), preferred_element_type=F32).astype(BF16)
    start = 0
    for ref in (seen_ref, last_ref):
        height, width = ref.shape
        flat = lax.broadcasted_iota(jnp.int32, (ins, width), 0) == (
            (lax.broadcasted_iota(jnp.int32, (ins, width), 1) + start) >> 4)
        full = jnp.dot(half, flat.astype(BF16), preferred_element_type=F32)
        same = (lax.broadcasted_iota(jnp.int32, ref.shape, 0) & (ROWS - 1)) == (
            lax.broadcasted_iota(jnp.int32, ref.shape, 1) & (ROWS - 1))
        ref[...] = jnp.where(same, full, 0.0).astype(BF16)
        start += width
    bonds = jnp.concatenate([coupling_ref[n] for n in range(slots)], axis=1)

    def spread(tall_ref, wide_ref):
        half = jnp.dot(tall_ref[...], bonds, precision=lax.Precision.HIGHEST, preferred_element_type=F32)
        return jnp.dot(half, wide_ref[...], precision=lax.Precision.HIGHEST, preferred_element_type=F32)

    pair_ref[...] = (spread(first_ref, wide_first_ref) * spread(second_ref, wide_second_ref)).astype(BF16)


def tables(pos, phonon, offsets, coupling, e_dev):
    slots, orbs = coupling.shape[0], coupling.shape[1]
    moms = phonon.shape[2]
    rel, mom = mixing_index(e_dev)
    pairs = np.arange(orbs * orbs)
    picks = [(index[:, None] == np.arange(orbs)).astype(np.float32) for index in (pairs // orbs, pairs % orbs)]
    wide = [np.kron(np.eye(slots, dtype=np.float32), pick.T) for pick in picks]
    return call(
        functools.partial(tables_kernel, moms),
        [((rel.shape[0] * ROWS, n * e_dev * ROWS), BF16) for n in (sum(len(p) for _, p in x) for x in (SEEN, LAST))]
        + [((orbs * orbs, slots * orbs * orbs), BF16)],
        pos, offsets, phonon, coupling, *map(jnp.asarray, (rel, mom, *picks, *wide)),
        cost=TABLES,
    )


def cut_kernel(groups, pos_ref, near_ref, green_ref, own_ref, give_ref, far_ref, home_ref):
    e_dev, pairs, _ = green_ref.shape
    rows = e_dev * pairs
    z, way = pos_ref[0], pos_ref[1]
    first = (2 * z + ((1 - way) >> 1)) * LANES
    steps = (near_ref[...] - first - lax.broadcasted_iota(jnp.int32, near_ref.shape, 1)).astype(F32)
    steps = jnp.concatenate([steps, jnp.zeros((ROWS - steps.shape[0], LANES), F32)], axis=0).astype(BF16)

    def put(ref, at, distance):
        group = (z + distance) & (groups - 1)
        for chunk in range(2):
            start = pl.multiple_of((chunk * groups + group) * LANES, LANES)
            ref[at, chunk * rows : (chunk + 1) * rows, :] = green_ref[:, :, pl.ds(start, LANES)].reshape(rows, LANES)
        ref[at, 2 * rows :, :] = steps

    for i, j in enumerate(NEAR):
        put(own_ref, i, way * j)
        put(give_ref, i, -way * j)
    put(far_ref, 0, 4)
    put(home_ref, 0, 0)


def cut(pos, near, green, groups):
    height = 2 * green.shape[0] * green.shape[1] + ROWS
    outs = [((n, height, LANES), BF16) for n in (len(NEAR), len(NEAR), 1, 1)]
    return call(functools.partial(cut_kernel, groups), outs, pos, near, green)


def merge_kernel(chips, own_ref, got_ref, *refs):
    whole = refs[: len(refs) - len(chips) >> 1]
    outs = refs[len(whole) :]
    for out, j in zip(outs, chips):
        out[0] = own_ref[j - 1]
        out[1] = got_ref[j - 1]
    for out, ref in zip(outs[len(chips) :], whole):
        out[...] = ref[...]


def merge(own, got, chips, *whole, after=()):
    outs = [((2, *own.shape[1:]), BF16)] * len(chips) + [(x.shape, BF16) for x in whole]
    return call(functools.partial(merge_kernel, chips), outs, own, got, *whole, after=after)


def stack_kernel(*refs):
    blocks, (out_ref, near_ref) = refs[:-2], refs[-2:]
    rows = out_ref.shape[1]
    at = 0
    for block in blocks:
        for i in range(block.shape[0]):
            out_ref[at] = block[i, 0:rows, :]
            near_ref[at] = block[i, rows:, :]
            at += 1


def stack(*blocks):
    places = sum(b.shape[0] for b in blocks)
    outs = [((places, h, LANES), BF16) for h in (blocks[0].shape[1] - ROWS, ROWS)]
    return call(stack_kernel, outs, *blocks)


def mix_kernel(e_dev, chunk, fields, mix_ref, *refs):
    refs, sums, (kept_ref, other_ref) = refs[:fields], refs[fields:-2], refs[-2:]
    places, height, width = kept_ref.shape
    pairs = height // e_dev
    for g in range(pairs // ROWS):
        tiles = []
        for ref in refs:
            for i in range(ref.shape[0]):
                for e in range(e_dev):
                    tiles.append(ref[i, pl.ds(chunk * height + e * pairs + g * ROWS, ROWS), :])
        mixed = jnp.dot(mix_ref[...], jnp.concatenate(tiles, axis=0), preferred_element_type=F32)
        mixed = mixed.reshape(e_dev, 2, places, ROWS, width)
        for e in range(e_dev):
            rows = pl.ds(e * pairs + g * ROWS, ROWS)
            for i, out in enumerate((kept_ref, other_ref)):
                total = mixed[e, i] + sums[i][:, rows, :] if sums else mixed[e, i]
                out[:, rows, :] = total.astype(out.dtype)


def mix(matrix, fields, chunk, e_dev, sums=(), after=()):
    shape = (len(PLACES), fields[0].shape[1] // 2, LANES)
    outs = [(shape, F32), (shape, BF16 if sums else F32)]
    return call(functools.partial(mix_kernel, e_dev, chunk, len(fields)), outs, matrix, *fields, *sums, after=after)


def add_kernel(kept_ref, got_ref, far, three, two, one, home):
    at = 0
    for out in (one, two, home, three, far):
        for i in range(out.shape[0]):
            out[i] = (kept_ref[at] + got_ref[at].astype(F32)).astype(BF16)
            at += 1


def add(kept, got, after=()):
    return call(add_kernel, [((n, *kept.shape[1:]), BF16) for n in (1, 2, 2, 2, 1)], kept, got, after=after)


def pick_kernel(*refs):
    blocks, extra, out = refs[: len(NEAR)], refs[len(NEAR) : -1], refs[-1]
    rows = blocks[0].shape[1]
    for i, block in enumerate(blocks):
        out[i * rows : (i + 1) * rows, :] = block[1]
    at = len(NEAR) * rows
    for near in extra:
        for i in range(near.shape[0]):
            out[at : at + near.shape[1], :] = near[i]
            at += near.shape[1]


def pick(blocks, *extra, after=()):
    height = len(NEAR) * blocks[1].shape[1] + sum(x.shape[0] * x.shape[1] for x in extra)
    return call(pick_kernel, [((height, LANES), BF16)], *blocks[3:0:-1], *extra, after=(blocks[0], *after))[0]


def gather_line(pos_ref, groups, line, base, far_ref, three_ref, two_ref, one_ref, home_ref, given_ref):
    z, way = pos_ref[0], pos_ref[1]
    rows = far_ref.shape[1]

    def put(block, distance):
        group = (z + distance) & (groups - 1)
        line[:, pl.ds(pl.multiple_of(base + group * LANES, LANES), LANES)] = block

    for i, (j, ref) in enumerate(zip(NEAR, (one_ref, two_ref, three_ref))):
        put(ref[0], -way * j)
        put(given_ref[i * rows : (i + 1) * rows, :], way * j)
    put(far_ref[0], 4)
    put(home_ref[0], 0)


def sum_block(line, window_at, near, pair_ref, e_dev):
    slots, pairs = pair_ref.shape[1] // pair_ref.shape[0], pair_ref.shape[0]
    place = lax.broadcasted_iota(jnp.int32, (SPAN, LANES), 0) - lax.broadcasted_iota(jnp.int32, (SPAN, LANES), 1) - PAD
    near = near.astype(F32).astype(jnp.int32)
    hits = [(place == near[n : n + 1, :]).astype(BF16) for n in range(slots)]
    window = line[:, pl.ds(window_at, SPAN)]
    taken = jnp.dot(window, jnp.concatenate(hits, axis=1), preferred_element_type=F32).astype(BF16)
    columns = [
        jnp.concatenate([taken[e * pairs : (e + 1) * pairs, n * LANES : (n + 1) * LANES] for n in range(slots)], axis=0)
        for e in range(e_dev)
    ]
    return jnp.dot(pair_ref[...], jnp.concatenate(columns, axis=1), preferred_element_type=F32).astype(BF16)


def first_kernel(groups, pos_ref, pair_ref, early_ref, late_ref, *refs):
    blocks, (out_ref, nears, tail, line, seen) = refs[:6], refs[6:]
    e_dev, pairs, atoms = out_ref.shape
    rows = e_dev * pairs
    z, way = pos_ref[0], pos_ref[1]
    core = (1 - way) >> 1

    def rank(distance, parity):
        return 2 * ((z + distance) & (groups - 1)) + parity

    at = len(NEAR) * rows
    for i, (j, other) in enumerate(PLACES):
        nears[rank(-way * j, core + way * other)] = early_ref[i] if i < len(EARLY) else late_ref[i - len(EARLY)]
        nears[rank(way * j, core + way - way * other)] = blocks[5][at : at + ROWS, :]
        at += ROWS
    gather_line(pos_ref, groups, seen, 0, *blocks)
    tail[...] = seen[:, groups * LANES - LANES - PAD :]
    line[:, 0:LANES] = jnp.zeros((rows, LANES), BF16)
    line[:, PAD : PAD + groups * LANES] = seen[...]

    def step(b, carry):
        start = pl.multiple_of(b * LANES, LANES)
        total = sum_block(line, start, nears[b], pair_ref, e_dev)
        for e in range(e_dev):
            out_ref[e, :, pl.ds(start, LANES)] = total[:, e * LANES : (e + 1) * LANES]
        return carry

    lax.fori_loop(0, atoms // LANES, step, 0, unroll=True)


def first_sum(pos, pair_maps, nears, blocks, groups, shape):
    rows = shape[0] * shape[1]
    return call(
        functools.partial(first_kernel, groups),
        [((*shape[:2], (groups - 1) * LANES), BF16), ((2 * groups, ROWS, LANES), BF16), ((rows, LANES + PAD), BF16)],
        pos, pair_maps, *nears, *blocks,
        scratch=[((rows, groups * LANES + LANES), BF16), ((rows, groups * LANES), BF16)],
    )


def second_kernel(groups, pos_ref, pair_ref, nears, done_ref, tail_ref, *refs):
    blocks, (out_ref, line, seen) = refs[:6], refs[6:]
    e_dev, pairs, atoms = out_ref.shape
    rows = e_dev * pairs
    first = done_ref.shape[2] // LANES
    width = (groups + 1) * LANES
    out_ref[:, :, 0 : first * LANES] = done_ref[...]
    gather_line(pos_ref, groups, seen, 0, *blocks)
    line[:, width:] = jnp.zeros((rows, LANES), BF16)
    line[:, 0 : LANES + PAD] = tail_ref[...]
    line[:, LANES + PAD : PAD + width] = seen[...]

    def step(b, carry):
        start = pl.multiple_of(b * LANES, LANES)
        total = sum_block(line, start, nears[b + first], pair_ref, e_dev)
        for e in range(e_dev):
            out_ref[e, :, pl.ds(pl.multiple_of(start + first * LANES, LANES), LANES)] = total[:, e * LANES : (e + 1) * LANES]
        return carry

    lax.fori_loop(0, atoms // LANES - first, step, 0, unroll=True)


def second_sum(pos, pair_maps, nears, done, tail, blocks, groups, shape):
    rows = shape[0] * shape[1]
    return call(
        functools.partial(second_kernel, groups),
        [(shape, BF16)],
        pos, pair_maps, nears, done, tail, *blocks,
        scratch=[((rows, (groups + 2) * LANES), BF16), ((rows, groups * LANES), BF16)],
    )[0]


def swap(x):
    return lax.ppermute(x, "core", [(0, 1), (1, 0)])


def round_ring(x, j):
    groups = lax.axis_size("z")
    pairs = [(2 * z + c, 2 * ((z + (j if c == 0 else -j)) % groups) + c) for z in range(groups) for c in range(2)]
    return lax.ppermute(x, KMOM, pairs)


def exchange(far, three, two, one, home):
    return [round_ring(far, 4), round_ring(three, 3), round_ring(two, 2), round_ring(one, 1), home]


def body(green_blocks, phonon, offsets, neighbours, coupling):
    groups, tiles = lax.axis_size("z"), lax.axis_size("energy")
    green = green_blocks[:, 0]
    e_dev, pairs, atoms = green.shape
    rows = e_dev * pairs
    core = lax.axis_index("core")
    pos = jnp.stack([lax.axis_index("z"), 1 - 2 * core])
    forward = [(i, i + 1) for i in range(tiles - 1)]
    backward = [(i + 1, i) for i in range(tiles - 1)]
    own, give, far, home = cut(pos, neighbours.T, green, groups)
    far, three, two, one, home = exchange(far, *merge(own, swap(give), (3, 2, 1)), home)
    parts = [stack(one, two, home), stack(three, far)]
    fields, near = zip(*parts)
    low = [lax.ppermute(x, "energy", forward) for x in fields]
    high = [lax.ppermute(x, "energy", backward) for x in fields]
    seen, last, pair_maps = tables(pos, phonon, offsets, coupling, e_dev)
    sums = [mix(seen, (low[0], fields[0], high[0], fields[1]), chunk, e_dev) for chunk in range(2)]
    backs = []
    for chunk in range(2):
        kept, other = mix(last, (low[1], high[1]), chunk, e_dev, sums[chunk], after=sums[1][:1])
        backs.append(exchange(*add(kept, swap(other))))
    blocks = [*backs[0], swap(pick(backs[0], *near))]
    done, nears, tail = first_sum(pos, pair_maps, near, blocks, groups, green.shape)
    blocks = [*backs[1], swap(pick(backs[1]))]
    return second_sum(pos, pair_maps, nears, done, tail, blocks, groups, green.shape)[:, None]


def solution(mesh):
    torus = Mesh(mesh.devices.reshape(mesh.shape["energy"], -1, 2), ("energy", *KMOM))
    placed = (P("energy", KMOM, None, None), P(), P(), P(KMOM, None), P())
    return jax.shard_map(body, mesh=torus, in_specs=placed, out_specs=P("energy", KMOM, None, None), check_vma=False)
```

```python
import functools

import jax
import jax.numpy as jnp
import numpy as np
from jax import lax
from jax.experimental import pallas as pl
from jax.experimental.pallas import tpu as pltpu
from jax.sharding import Mesh
from jax.sharding import PartitionSpec as P

OFFSET = 2
TAPS = 2 * OFFSET + 1
ROWS = 16
COST = 1
TABLES = 20000000000
PARTS = 1
LANES = 128
SPAN = 2 * LANES
PAD = LANES // 2
KMOM = ("z", "core")
VMEM = pl.BlockSpec(memory_space=pltpu.VMEM)
SMEM = pl.BlockSpec(memory_space=pltpu.SMEM)
BF16, F32 = jnp.bfloat16, jnp.float32

NEAR = (1, 2, 3)
EARLY = ((1, 0), (1, 1), (2, 0), (2, 1), (0, 0))
LATE = ((3, 0), (3, 1), (4, 0))
PLACES = EARLY + LATE
SEEN = ((-1, EARLY), (0, EARLY), (1, EARLY), (0, LATE))
LAST = ((-1, LATE), (1, LATE))


def call(kernel, outs, *args, scratch=(), after=(), cost=COST):
    def run(*refs):
        kernel(*refs[: len(args)], *refs[len(args) + len(after) :])

    return pl.pallas_call(
        run,
        out_shape=[jax.ShapeDtypeStruct(shape, dtype) for shape, dtype in outs],
        in_specs=[SMEM if a.ndim == 1 else VMEM for a in args] + [pl.BlockSpec(memory_space=pl.ANY)] * len(after),
        out_specs=[VMEM] * len(outs),
        scratch_shapes=[pltpu.VMEM(shape, dtype) for shape, dtype in scratch],
        cost_estimate=pl.CostEstimate(flops=cost, bytes_accessed=1, transcendentals=0),
        compiler_params=pltpu.CompilerParams(vmem_limit_bytes=40 * 2**20),
    )(*args, *after)


def mixing_index(e_dev):
    columns = [(tile, place, e) for parts in (SEEN, LAST) for tile, part in parts for place in part for e in range(e_dev)]
    rel = np.zeros((e_dev, 2, len(PLACES), len(columns)), np.int32)
    mom = np.zeros_like(rel)
    for at, (tile, (j_from, from_other), e_in) in enumerate(columns):
        for e_out in range(e_dev):
            rel[e_out, ..., at] = tile * e_dev + e_in - e_out + OFFSET
        for d, (j_to, to_other) in enumerate(PLACES):
            mom[:, 0, d, at] = 2 * (j_to + j_from) + to_other - from_other
            mom[:, 1, d, at] = 2 * (j_from - j_to) + 1 - to_other - from_other
    return rel.reshape(-1, len(columns)), mom.reshape(-1, len(columns))


def tables_kernel(moms, pos_ref, offsets_ref, phonon_ref, coupling_ref, rel_ref, mom_ref, first_ref, second_ref,
                  wide_first_ref, wide_second_ref, seen_ref, last_ref, pair_ref):
    slots = coupling_ref.shape[0]
    taps = jnp.zeros((8, moms), F32)
    row = lax.broadcasted_iota(jnp.int32, (8, moms), 0)
    for s in range(2):
        for w in range(phonon_ref.shape[1]):
            hit = row == (2 * s - 1) * offsets_ref[w] + OFFSET
            taps = taps + jnp.where(hit, phonon_ref[s, w : w + 1, :], 0.0)
    taps = taps.astype(BF16).astype(F32)
    rel, mom = rel_ref[...], (mom_ref[...] * pos_ref[1]) & (moms - 1)
    table = jnp.zeros(rel.shape, F32)
    for r in range(TAPS):
        for q in range(moms):
            table = jnp.where((rel == r) & (mom == q), taps[r : r + 1, q : q + 1], table)
    outs, ins = table.shape
    tall = (lax.broadcasted_iota(jnp.int32, (outs * ROWS, outs), 0) >> 4) == lax.broadcasted_iota(
        jnp.int32, (outs * ROWS, outs), 1)
    half = jnp.dot(tall.astype(BF16), table.astype(BF16), preferred_element_type=F32).astype(BF16)
    start = 0
    for ref in (seen_ref, last_ref):
        height, width = ref.shape
        flat = lax.broadcasted_iota(jnp.int32, (ins, width), 0) == (
            (lax.broadcasted_iota(jnp.int32, (ins, width), 1) + start) >> 4)
        full = jnp.dot(half, flat.astype(BF16), preferred_element_type=F32)
        same = (lax.broadcasted_iota(jnp.int32, ref.shape, 0) & (ROWS - 1)) == (
            lax.broadcasted_iota(jnp.int32, ref.shape, 1) & (ROWS - 1))
        ref[...] = jnp.where(same, full, 0.0).astype(BF16)
        start += width
    bonds = jnp.concatenate([coupling_ref[n] for n in range(slots)], axis=1)

    def spread(tall_ref, wide_ref):
        half = jnp.dot(tall_ref[...], bonds, precision=lax.Precision.HIGHEST, preferred_element_type=F32)
        return jnp.dot(half, wide_ref[...], precision=lax.Precision.HIGHEST, preferred_element_type=F32)

    pair_ref[...] = (spread(first_ref, wide_first_ref) * spread(second_ref, wide_second_ref)).astype(BF16)


def tables(pos, phonon, offsets, coupling, e_dev):
    slots, orbs = coupling.shape[0], coupling.shape[1]
    moms = phonon.shape[2]
    rel, mom = mixing_index(e_dev)
    pairs = np.arange(orbs * orbs)
    picks = [(index[:, None] == np.arange(orbs)).astype(np.float32) for index in (pairs // orbs, pairs % orbs)]
    wide = [np.kron(np.eye(slots, dtype=np.float32), pick.T) for pick in picks]
    return call(
        functools.partial(tables_kernel, moms),
        [((rel.shape[0] * ROWS, n * e_dev * ROWS), BF16) for n in (sum(len(p) for _, p in x) for x in (SEEN, LAST))]
        + [((orbs * orbs, slots * orbs * orbs), BF16)],
        pos, offsets, phonon, coupling, *map(jnp.asarray, (rel, mom, *picks, *wide)),
        cost=TABLES,
    )


def cut_kernel(groups, pos_ref, near_ref, green_ref, own_ref, give_ref, far_ref, home_ref):
    e_dev, pairs, _ = green_ref.shape
    rows = e_dev * pairs
    z, way = pos_ref[0], pos_ref[1]
    first = (2 * z + ((1 - way) >> 1)) * LANES
    steps = (near_ref[...] - first - lax.broadcasted_iota(jnp.int32, near_ref.shape, 1)).astype(F32)
    steps = jnp.concatenate([steps, jnp.zeros((ROWS - steps.shape[0], LANES), F32)], axis=0).astype(BF16)

    def put(ref, at, distance):
        group = (z + distance) & (groups - 1)
        for chunk in range(2):
            start = pl.multiple_of((chunk * groups + group) * LANES, LANES)
            ref[at, chunk * rows : (chunk + 1) * rows, :] = green_ref[:, :, pl.ds(start, LANES)].reshape(rows, LANES)
        ref[at, 2 * rows :, :] = steps

    for i, j in enumerate(NEAR):
        put(own_ref, i, way * j)
        put(give_ref, i, -way * j)
    put(far_ref, 0, 4)
    put(home_ref, 0, 0)


def cut(pos, near, green, groups):
    height = 2 * green.shape[0] * green.shape[1] + ROWS
    outs = [((n, height, LANES), BF16) for n in (len(NEAR), len(NEAR), 1, 1)]
    return call(functools.partial(cut_kernel, groups), outs, pos, near, green)


def merge_kernel(chips, own_ref, got_ref, *refs):
    whole = refs[: len(refs) - len(chips) >> 1]
    outs = refs[len(whole) :]
    for out, j in zip(outs, chips):
        out[0] = own_ref[j - 1]
        out[1] = got_ref[j - 1]
    for out, ref in zip(outs[len(chips) :], whole):
        out[...] = ref[...]


def merge(own, got, chips, *whole, after=()):
    outs = [((2, *own.shape[1:]), BF16)] * len(chips) + [(x.shape, BF16) for x in whole]
    return call(functools.partial(merge_kernel, chips), outs, own, got, *whole, after=after)


def stack_kernel(*refs):
    blocks, (out_ref, near_ref) = refs[:-2], refs[-2:]
    rows = out_ref.shape[1]
    at = 0
    for block in blocks:
        for i in range(block.shape[0]):
            out_ref[at] = block[i, 0:rows, :]
            near_ref[at] = block[i, rows:, :]
            at += 1


def stack(*blocks):
    places = sum(b.shape[0] for b in blocks)
    outs = [((places, h, LANES), BF16) for h in (blocks[0].shape[1] - ROWS, ROWS)]
    return call(stack_kernel, outs, *blocks)


def mix_kernel(e_dev, chunk, fields, mix_ref, *refs):
    refs, sums, (kept_ref, other_ref) = refs[:fields], refs[fields:-2], refs[-2:]
    places, height, width = kept_ref.shape
    pairs = height // e_dev
    for g in range(pairs // ROWS):
        tiles = []
        for ref in refs:
            for i in range(ref.shape[0]):
                for e in range(e_dev):
                    tiles.append(ref[i, pl.ds(chunk * height + e * pairs + g * ROWS, ROWS), :])
        mixed = jnp.dot(mix_ref[...], jnp.concatenate(tiles, axis=0), preferred_element_type=F32)
        mixed = mixed.reshape(e_dev, 2, places, ROWS, width)
        for e in range(e_dev):
            rows = pl.ds(e * pairs + g * ROWS, ROWS)
            for i, out in enumerate((kept_ref, other_ref)):
                total = mixed[e, i] + sums[i][:, rows, :] if sums else mixed[e, i]
                out[:, rows, :] = total.astype(out.dtype)


def mix(matrix, fields, chunk, e_dev, sums=(), after=()):
    shape = (len(PLACES), fields[0].shape[1] // 2, LANES)
    outs = [(shape, F32), (shape, BF16 if sums else F32)]
    return call(functools.partial(mix_kernel, e_dev, chunk, len(fields)), outs, matrix, *fields, *sums, after=after)


def add_kernel(kept_ref, got_ref, far, three, two, one, home):
    at = 0
    for out in (one, two, home, three, far):
        for i in range(out.shape[0]):
            out[i] = (kept_ref[at] + got_ref[at].astype(F32)).astype(BF16)
            at += 1


def add(kept, got, after=()):
    return call(add_kernel, [((n, *kept.shape[1:]), BF16) for n in (1, 2, 2, 2, 1)], kept, got, after=after)


def pick_kernel(*refs):
    blocks, extra, out = refs[: len(NEAR)], refs[len(NEAR) : -1], refs[-1]
    rows = blocks[0].shape[1]
    for i, block in enumerate(reversed(blocks)):
        out[i * rows : (i + 1) * rows, :] = block[1]
    at = len(NEAR) * rows
    for near in extra:
        for i in range(near.shape[0]):
            out[at : at + near.shape[1], :] = near[i]
            at += near.shape[1]


def pick(blocks, *extra, after=()):
    height = len(NEAR) * blocks[1].shape[1] + sum(x.shape[0] * x.shape[1] for x in extra)
    return call(pick_kernel, [((height, LANES), BF16)], *blocks[1:4], *extra, after=(blocks[0], *after))[0]


def gather_line(pos_ref, groups, line, base, far_ref, three_ref, two_ref, one_ref, home_ref, given_ref):
    z, way = pos_ref[0], pos_ref[1]
    rows = far_ref.shape[1]

    def put(block, distance):
        group = (z + distance) & (groups - 1)
        line[:, pl.ds(pl.multiple_of(base + group * LANES, LANES), LANES)] = block

    for i, (j, ref) in enumerate(zip(NEAR, (one_ref, two_ref, three_ref))):
        put(ref[0], -way * j)
        put(given_ref[i * rows : (i + 1) * rows, :], way * j)
    put(far_ref[0], 4)
    put(home_ref[0], 0)


def sum_block(line, window_at, near, pair_ref, e_dev):
    slots, pairs = pair_ref.shape[1] // pair_ref.shape[0], pair_ref.shape[0]
    place = lax.broadcasted_iota(jnp.int32, (SPAN, LANES), 0) - lax.broadcasted_iota(jnp.int32, (SPAN, LANES), 1) - PAD
    near = near.astype(F32).astype(jnp.int32)
    hits = [(place == near[n : n + 1, :]).astype(BF16) for n in range(slots)]
    window = line[:, pl.ds(window_at, SPAN)]
    taken = jnp.dot(window, jnp.concatenate(hits, axis=1), preferred_element_type=F32).astype(BF16)
    columns = [
        jnp.concatenate([taken[e * pairs : (e + 1) * pairs, n * LANES : (n + 1) * LANES] for n in range(slots)], axis=0)
        for e in range(e_dev)
    ]
    return jnp.dot(pair_ref[...], jnp.concatenate(columns, axis=1), preferred_element_type=F32).astype(BF16)


def first_kernel(groups, pos_ref, pair_ref, early_ref, late_ref, *refs):
    blocks, (out_ref, nears, tail, line, seen) = refs[:6], refs[6:]
    e_dev, pairs, atoms = out_ref.shape
    rows = e_dev * pairs
    z, way = pos_ref[0], pos_ref[1]
    core = (1 - way) >> 1

    def rank(distance, parity):
        return 2 * ((z + distance) & (groups - 1)) + parity

    at = len(NEAR) * rows
    for i, (j, other) in enumerate(PLACES):
        nears[rank(-way * j, core + way * other)] = early_ref[i] if i < len(EARLY) else late_ref[i - len(EARLY)]
        nears[rank(way * j, core + way - way * other)] = blocks[5][at : at + ROWS, :]
        at += ROWS
    gather_line(pos_ref, groups, seen, 0, *blocks)
    tail[...] = seen[:, groups * LANES - LANES - PAD :]
    line[:, 0:LANES] = jnp.zeros((rows, LANES), BF16)
    line[:, PAD : PAD + groups * LANES] = seen[...]

    def step(b, carry):
        start = pl.multiple_of(b * LANES, LANES)
        total = sum_block(line, start, nears[b], pair_ref, e_dev)
        for e in range(e_dev):
            out_ref[e, :, pl.ds(start, LANES)] = total[:, e * LANES : (e + 1) * LANES]
        return carry

    lax.fori_loop(0, atoms // LANES, step, 0, unroll=True)


def first_sum(pos, pair_maps, nears, blocks, groups, shape):
    rows = shape[0] * shape[1]
    return call(
        functools.partial(first_kernel, groups),
        [((*shape[:2], (groups - 1) * LANES), BF16), ((2 * groups, ROWS, LANES), BF16), ((rows, LANES + PAD), BF16)],
        pos, pair_maps, *nears, *blocks,
        scratch=[((rows, groups * LANES + LANES), BF16), ((rows, groups * LANES), BF16)],
    )


def second_kernel(groups, pos_ref, pair_ref, nears, done_ref, tail_ref, *refs):
    blocks, (out_ref, line, seen) = refs[:6], refs[6:]
    e_dev, pairs, atoms = out_ref.shape
    rows = e_dev * pairs
    first = done_ref.shape[2] // LANES
    width = (groups + 1) * LANES
    out_ref[:, :, 0 : first * LANES] = done_ref[...]
    gather_line(pos_ref, groups, seen, 0, *blocks)
    line[:, width:] = jnp.zeros((rows, LANES), BF16)
    line[:, 0 : LANES + PAD] = tail_ref[...]
    line[:, LANES + PAD : PAD + width] = seen[...]

    def step(b, carry):
        start = pl.multiple_of(b * LANES, LANES)
        total = sum_block(line, start, nears[b + first], pair_ref, e_dev)
        for e in range(e_dev):
            out_ref[e, :, pl.ds(pl.multiple_of(start + first * LANES, LANES), LANES)] = total[:, e * LANES : (e + 1) * LANES]
        return carry

    lax.fori_loop(0, atoms // LANES - first, step, 0, unroll=True)


def second_sum(pos, pair_maps, nears, done, tail, blocks, groups, shape):
    rows = shape[0] * shape[1]
    return call(
        functools.partial(second_kernel, groups),
        [(shape, BF16)],
        pos, pair_maps, nears, done, tail, *blocks,
        scratch=[((rows, (groups + 2) * LANES), BF16), ((rows, groups * LANES), BF16)],
    )[0]


def swap(x):
    return lax.ppermute(x, "core", [(0, 1), (1, 0)])


def round_ring(x, j):
    groups = lax.axis_size("z")
    pairs = [(2 * z + c, 2 * ((z + (j if c == 0 else -j)) % groups) + c) for z in range(groups) for c in range(2)]
    return lax.ppermute(x, KMOM, pairs)


def exchange(far, three, two, one, home):
    return [round_ring(far, 4), round_ring(three, 3), round_ring(two, 2), round_ring(one, 1), home]


def body(green_blocks, phonon, offsets, neighbours, coupling):
    groups, tiles = lax.axis_size("z"), lax.axis_size("energy")
    green = green_blocks[:, 0]
    e_dev, pairs, atoms = green.shape
    rows = e_dev * pairs
    core = lax.axis_index("core")
    pos = jnp.stack([lax.axis_index("z"), 1 - 2 * core])
    forward = [(i, i + 1) for i in range(tiles - 1)]
    backward = [(i + 1, i) for i in range(tiles - 1)]
    own, give, far, home = cut(pos, neighbours.T, green, groups)
    far, three, two, one, home = exchange(far, *merge(own, swap(give), (3, 2, 1)), home)
    parts = [stack(one, two, home), stack(three, far)]
    fields, near = zip(*parts)
    low = [lax.ppermute(x, "energy", forward) for x in fields]
    high = [lax.ppermute(x, "energy", backward) for x in fields]
    seen, last, pair_maps = tables(pos, phonon, offsets, coupling, e_dev)
    sums = [mix(seen, (low[0], fields[0], high[0], fields[1]), chunk, e_dev) for chunk in range(2)]
    backs = []
    for chunk in range(2):
        kept, other = mix(last, (low[1], high[1]), chunk, e_dev, sums[chunk], after=sums[1][:1])
        backs.append(exchange(*add(kept, swap(other))))
    blocks = [*backs[0], swap(pick(backs[0], *near))]
    done, nears, tail = first_sum(pos, pair_maps, near, blocks, groups, green.shape)
    blocks = [*backs[1], swap(pick(backs[1]))]
    return second_sum(pos, pair_maps, nears, done, tail, blocks, groups, green.shape)[:, None]


def solution(mesh):
    torus = Mesh(mesh.devices.reshape(mesh.shape["energy"], -1, 2), ("energy", *KMOM))
    placed = (P("energy", KMOM, None, None), P(), P(), P(KMOM, None), P())
    return jax.shard_map(body, mesh=torus, in_specs=placed, out_specs=P("energy", KMOM, None, None), check_vma=False)
```
